256 devices in a mesh: grp: 8 (over x, core), dev: 32 (over z, y).
Axes of the slice: x: 4, y: 4, z: 8, core: 2. Of those that a mesh axis runs over, the one named last changes fastest.
Arguments:
- embed_source: float32 [131072, 256], P(('grp', 'dev')), may hold values from -1 to 1
- embed_target: float32 [131072, 256], P(('grp', 'dev')), may hold values from -1 to 1
- mass_source: float32 [131072], P(('grp', 'dev')), may hold values from 0.3 to 9
- mass_target: float32 [131072], P(('grp', 'dev')), may hold values from 0.3 to 9
- start_source: float32 [131072, 256], P(('grp', 'dev')), may hold values from 0.5 to 8
- start_target: float32 [131072, 256], P(('grp', 'dev')), may hold values from 0.5 to 8
Outputs:
- factor_source: float32 [131072, 256], P(('grp', 'dev'))
- factor_target: float32 [131072, 256], P(('grp', 'dev'))
- inner_marginal: float32 [256], replicated
The draws below stay inside these ranges and needn't reach their ends.
All inputs are finite; a program needn't handle non-finite values. Where the reference program divides by a largest or mean magnitude, that divisor is 1e-20 or more.
Results may differ from the reference program's by a relative error of at most 0.0003.
Values sent between devices are 32-bit elements; how exact they have to be, the bound alone decides.
No kernel may reach another device: no remote copies, remote signals or barrier semaphores. Data moves between devices by JAX's collectives and lax.ppermute only.
A program may use at most 64 MiB of HBM per device.

```python
import math
import jax
import jax.numpy as jnp
from jax import lax

D = 256
RANK = 256
OUTER = 2
INNER = 8
POINTS = 131072


def shared_centres(key):
    return jax.random.truncated_normal(jax.random.fold_in(key, 101), -4.0, 4.0, (RANK, D), jnp.float32) * (0.8 / math.sqrt(D))


def shared_labels(key, salt):
    return jax.random.randint(jax.random.fold_in(key, salt), (POINTS,), 0, RANK)


def draw_embed_source(key, part):
    centres = shared_centres(key)
    labels = shared_labels(key, 102)
    key = jax.random.fold_in(key, 1)
    noise_key, scale_key = jax.random.split(key)
    noise = jax.random.truncated_normal(noise_key, -4.0, 4.0, (POINTS, D), jnp.float32) * (0.5 / math.sqrt(D))
    scale = jnp.exp(jax.random.uniform(scale_key, (POINTS, 1), jnp.float32, math.log(0.6), math.log(1.6)))
    return jnp.clip(scale * (centres[labels] + noise), -1.0, 1.0)


def draw_embed_target(key, part):
    centres = shared_centres(key)
    labels = shared_labels(key, 103)
    key = jax.random.fold_in(key, 2)
    noise_key, scale_key = jax.random.split(key)
    noise = jax.random.truncated_normal(noise_key, -4.0, 4.0, (POINTS, D), jnp.float32) * (0.5 / math.sqrt(D))
    scale = jnp.exp(jax.random.uniform(scale_key, (POINTS, 1), jnp.float32, math.log(0.6), math.log(1.6)))
    return jnp.clip(scale * (centres[labels] + noise), -1.0, 1.0)


def draw_mass_source(key, part):
    key = jax.random.fold_in(key, 5)
    rise = 3.0 ** (jnp.arange(POINTS, dtype=jnp.float32) / POINTS)
    base = jnp.exp(jax.random.uniform(key, (POINTS,), jnp.float32, math.log(0.5), math.log(2.0)))
    return base * rise


def draw_mass_target(key, part):
    key = jax.random.fold_in(key, 6)
    rise = 3.0 ** (jnp.arange(POINTS, dtype=jnp.float32) / POINTS)
    base = jnp.exp(jax.random.uniform(key, (POINTS,), jnp.float32, math.log(0.5), math.log(2.0)))
    return base * rise


def blocked_start(key, quarter):
    low_key, high_key = jax.random.split(key)
    low = jnp.exp(jax.random.uniform(low_key, (POINTS, RANK), jnp.float32, math.log(0.5), math.log(0.8)))
    high = jnp.exp(jax.random.uniform(high_key, (POINTS, RANK), jnp.float32, math.log(5.0), math.log(8.0)))
    column = jnp.arange(RANK, dtype=jnp.int32) // (RANK // 4)
    inside = quarter[:, None] == column[None, :]
    return jnp.where(inside, high, low)


def draw_start_source(key, part):
    key = jax.random.fold_in(key, 3)
    quarter = jnp.arange(POINTS, dtype=jnp.int32) * 4 // POINTS
    return blocked_start(key, quarter)


def draw_start_target(key, part):
    key = jax.random.fold_in(key, 4)
    quarter = 3 - jnp.arange(POINTS, dtype=jnp.int32) * 4 // POINTS
    return blocked_start(key, quarter)


def setup_inputs(seed: int = 0) -> dict:
    seeds = jax.random.split(jax.random.key(seed), 7)
    embed_source = draw_embed_source(jax.random.fold_in(seeds[6], 71), 0)
    embed_target = draw_embed_target(jax.random.fold_in(seeds[6], 71), 0)
    mass_source = draw_mass_source(jax.random.fold_in(seeds[6], 71), 0)
    mass_target = draw_mass_target(jax.random.fold_in(seeds[6], 71), 0)
    start_source = draw_start_source(jax.random.fold_in(seeds[6], 71), 0)
    start_target = draw_start_target(jax.random.fold_in(seeds[6], 71), 0)
    return dict(embed_source=embed_source, embed_target=embed_target, mass_source=mass_source, mass_target=mass_target, start_source=start_source, start_target=start_target)


HIGH = lax.Precision.HIGHEST


def reference(embed_source, embed_target, mass_source, mass_target, start_source, start_target):
    source_mass = mass_source / jnp.sum(mass_source)
    target_mass = mass_target / jnp.sum(mass_target)
    left = start_source * (source_mass / jnp.sum(start_source, 1))[:, None]
    right = start_target * (target_mass / jnp.sum(start_target, 1))[:, None]
    middle = jnp.full((RANK,), 1.0 / RANK, jnp.float32)
    norm_source = jnp.sum(embed_source * embed_source, 1)
    norm_target = jnp.sum(embed_target * embed_target, 1)
    for outer in range(OUTER):
        cross_source = jnp.dot(embed_source.T, left, precision=HIGH)
        cross_target = jnp.dot(embed_target.T, right, precision=HIGH)
        heavy_source = jnp.dot(norm_source, left, precision=HIGH)
        plain_source = jnp.sum(left, 0)
        heavy_target = jnp.dot(norm_target, right, precision=HIGH)
        plain_target = jnp.sum(right, 0)
        cost_right = norm_source[:, None] * plain_target[None, :] + heavy_target[None, :] - 2.0 * jnp.dot(embed_source, cross_target, precision=HIGH)
        cost_left = norm_target[:, None] * plain_source[None, :] + heavy_source[None, :] - 2.0 * jnp.dot(embed_target, cross_source, precision=HIGH)
        grad_left = cost_right / middle[None, :]
        grad_right = cost_left / middle[None, :]
        diagonal = jnp.sum(left * cost_right, 0)
        grad_middle = -diagonal / (middle * middle)
        peak = jnp.maximum(jnp.maximum(jnp.max(jnp.abs(grad_left)), jnp.max(jnp.abs(grad_right))), jnp.max(jnp.abs(grad_middle)))
        rate = 30.0 / (peak * peak + 1e-6)
        kernel_left = left * jnp.exp(-rate * grad_left)
        kernel_right = right * jnp.exp(-rate * grad_right)
        kernel_middle = middle * jnp.exp(-rate * grad_middle)
        scale_left = jnp.ones((RANK,), jnp.float32)
        scale_right = jnp.ones((RANK,), jnp.float32)
        for inner in range(INNER):
            row_left = source_mass / jnp.dot(kernel_left, scale_left, precision=HIGH)
            row_right = target_mass / jnp.dot(kernel_right, scale_right, precision=HIGH)
            marg_left = jnp.dot(row_left, kernel_left, precision=HIGH)
            marg_right = jnp.dot(row_right, kernel_right, precision=HIGH)
            middle = jnp.cbrt(kernel_middle * scale_left * marg_left * scale_right * marg_right)
            scale_left = middle / marg_left
            scale_right = middle / marg_right
        left = row_left[:, None] * kernel_left * scale_left[None, :]
        right = row_right[:, None] * kernel_right * scale_right[None, :]
    factor = float(POINTS * RANK)
    return left * factor, right * factor, middle * float(RANK)
```

```python
import jax
import jax.numpy as jnp
from jax import lax
from jax.sharding import PartitionSpec as P

OUTER = 2
INNER = 8
AXES = ("grp", "dev")
HIGH = lax.Precision.HIGHEST


def contract_rows(a, b):
    return lax.dot_general(a, b, (((0,), (0,)), ((), ())), precision=HIGH, preferred_element_type=jnp.float32)


def exchange(value, axes, size):
    return lax.all_to_all(jnp.broadcast_to(value[None], (size,) + value.shape), axes, 0, 0)


def sum_all(value):
    value = jnp.sum(exchange(value, "grp", lax.axis_size("grp")), 0)
    return jnp.sum(exchange(value, "dev", lax.axis_size("dev")), 0)


def sum_columns(first, second, small):
    rank, width = first.shape
    count = lax.axis_size("grp") * lax.axis_size("dev")
    share = rank // count
    pad = jnp.zeros((rank, 128 - small.shape[0]), jnp.float32)
    packed = jnp.concatenate([first, second, small.T, pad], 1)
    total = packed.shape[1]
    part = jnp.sum(lax.all_to_all(packed.reshape(count, share, total), AXES, 0, 0), 0)
    full = exchange(part, AXES, count).reshape(rank, total)
    return full[:, :width], full[:, width : 2 * width], full[:, 2 * width : 2 * width + small.shape[0]].T


def max_all(value):
    count = lax.axis_size("grp") * lax.axis_size("dev")
    return jnp.max(exchange(jnp.broadcast_to(value, (2,)), AXES, count))


def local(embed_source, embed_target, mass_source, mass_target, start_source, start_target):
    rank = start_source.shape[1]
    norm_source = jnp.sum(embed_source * embed_source, 1)
    norm_target = jnp.sum(embed_target * embed_target, 1)
    left = start_source * (mass_source / jnp.sum(start_source, 1))[:, None]
    right = start_target * (mass_target / jnp.sum(start_target, 1))[:, None]
    middle = jnp.full((rank,), 1.0 / rank, jnp.float32)
    weights_left, weights_right = left, right
    for outer in range(OUTER):
        small = jnp.stack(
            [
                jnp.dot(norm_source, weights_left, precision=HIGH),
                jnp.sum(weights_left, 0),
                jnp.dot(norm_target, weights_right, precision=HIGH),
                jnp.sum(weights_right, 0),
                jnp.full((rank,), jnp.sum(mass_source)),
                jnp.full((rank,), jnp.sum(mass_target)),
            ]
        )
        cross_source, cross_target, small = sum_columns(
            contract_rows(weights_left, embed_source), contract_rows(weights_right, embed_target), small
        )
        if outer == 0:
            inverse_left = 1.0 / small[4]
            inverse_right = 1.0 / small[5]
            source_mass = mass_source * inverse_left[0]
            target_mass = mass_target * inverse_right[0]
            left = left * inverse_left[0]
            right = right * inverse_right[0]
        else:
            marg_left = small[1]
            marg_right = small[3]
            middle = jnp.cbrt(kernel_middle * scale_left * marg_left * scale_right * marg_right)
            inverse_left = middle / marg_left
            inverse_right = middle / marg_right
            left = weights_left * inverse_left[None, :]
            right = weights_right * inverse_right[None, :]
        cross_source = cross_source * inverse_left[:, None]
        cross_target = cross_target * inverse_right[:, None]
        heavy_source, plain_source = small[0] * inverse_left, small[1] * inverse_left
        heavy_target, plain_target = small[2] * inverse_right, small[3] * inverse_right
        diagonal = (
            heavy_source * plain_target + plain_source * heavy_target - 2.0 * jnp.sum(cross_source * cross_target, 1)
        )
        grad_middle = -diagonal / (middle * middle)
        over = 1.0 / middle
        grad_left = (
            norm_source[:, None] * (plain_target * over)[None, :]
            + (heavy_target * over)[None, :]
            - 2.0
            * lax.dot_general(
                embed_source, cross_target * over[:, None], (((1,), (1,)), ((), ())), precision=HIGH
            )
        )
        grad_right = (
            norm_target[:, None] * (plain_source * over)[None, :]
            + (heavy_source * over)[None, :]
            - 2.0
            * lax.dot_general(
                embed_target, cross_source * over[:, None], (((1,), (1,)), ((), ())), precision=HIGH
            )
        )
        peak = max_all(jnp.maximum(jnp.max(jnp.abs(grad_left)), jnp.max(jnp.abs(grad_right))))
        peak = jnp.maximum(peak, jnp.max(jnp.abs(grad_middle)))
        rate = 30.0 / (peak * peak + 1e-06)
        kernel_left = left * jnp.exp(-rate * grad_left)
        kernel_right = right * jnp.exp(-rate * grad_right)
        kernel_middle = middle * jnp.exp(-rate * grad_middle)
        scale_left = jnp.ones((rank,), jnp.float32)
        scale_right = jnp.ones((rank,), jnp.float32)
        for inner in range(INNER):
            row_left = source_mass / jnp.dot(kernel_left, scale_left, precision=HIGH)
            row_right = target_mass / jnp.dot(kernel_right, scale_right, precision=HIGH)
            if outer < OUTER - 1 and inner == INNER - 1:
                weights_left = row_left[:, None] * kernel_left
                weights_right = row_right[:, None] * kernel_right
                break
            margins = sum_all(
                jnp.stack(
                    [
                        jnp.dot(row_left, kernel_left, precision=HIGH),
                        jnp.dot(row_right, kernel_right, precision=HIGH),
                    ]
                )
            )
            marg_left = margins[0]
            marg_right = margins[1]
            middle = jnp.cbrt(kernel_middle * scale_left * marg_left * scale_right * marg_right)
            scale_left = middle / marg_left
            scale_right = middle / marg_right
    left = row_left[:, None] * kernel_left * scale_left[None, :]
    right = row_right[:, None] * kernel_right * scale_right[None, :]
    total_points = left.shape[0] * lax.axis_size("grp") * lax.axis_size("dev")
    factor = float(total_points * rank)
    return (left * factor, right * factor, middle * float(rank))


def solution(mesh):
    return jax.shard_map(
        local,
        mesh=mesh,
        in_specs=(
            P(AXES, None),
            P(AXES, None),
            P(AXES),
            P(AXES),
            P(AXES, None),
            P(AXES, None),
        ),
        out_specs=(P(AXES, None), P(AXES, None), P()),
        check_vma=False,
    )
```

```python
import jax
import jax.numpy as jnp
from jax import lax
from jax.sharding import Mesh, PartitionSpec as P

OUTER = 2
INNER = 8
AXES = ("x", "core", "z", "y")
HIGH = lax.Precision.HIGHEST


def contract_rows(a, b):
    return lax.dot_general(a, b, (((0,), (0,)), ((), ())), precision=HIGH, preferred_element_type=jnp.float32)


def exchange(value, axes, size):
    return lax.all_to_all(jnp.broadcast_to(value[None], (size,) + value.shape), axes, 0, 0)


def sum_all(value):
    value = jnp.sum(exchange(value, ("x", "core"), lax.axis_size(("x", "core"))), 0)
    return jnp.sum(exchange(value, ("z", "y"), lax.axis_size(("z", "y"))), 0)


def sum_columns(first, second, small):
    rank, width = first.shape
    plane = ("x", "core", "y")
    count = lax.axis_size(plane)
    pad = jnp.zeros((rank, 128 - small.shape[0]), jnp.float32)
    packed = jnp.concatenate([first, second, small.T, pad], 1)
    total = packed.shape[1]
    part = jnp.sum(lax.all_to_all(packed.reshape(count, rank // count, total), plane, 0, 0), 0)
    part = jnp.sum(exchange(part, "z", lax.axis_size("z")), 0)
    full = exchange(part, plane, count).reshape(rank, total)
    return full[:, :width], full[:, width : 2 * width], full[:, 2 * width : 2 * width + small.shape[0]].T


def max_all(value):
    count = lax.axis_size(AXES)
    return jnp.max(exchange(jnp.broadcast_to(value, (2,)), AXES, count))


def local(embed_source, embed_target, mass_source, mass_target, start_source, start_target):
    rank = start_source.shape[1]
    norm_source = jnp.sum(embed_source * embed_source, 1)
    norm_target = jnp.sum(embed_target * embed_target, 1)
    left = start_source * (mass_source / jnp.sum(start_source, 1))[:, None]
    right = start_target * (mass_target / jnp.sum(start_target, 1))[:, None]
    middle = jnp.full((rank,), 1.0 / rank, jnp.float32)
    weights_left, weights_right = left, right
    for outer in range(OUTER):
        small = jnp.stack(
            [
                jnp.dot(norm_source, weights_left, precision=HIGH),
                jnp.sum(weights_left, 0),
                jnp.dot(norm_target, weights_right, precision=HIGH),
                jnp.sum(weights_right, 0),
                jnp.full((rank,), jnp.sum(mass_source)),
                jnp.full((rank,), jnp.sum(mass_target)),
            ]
        )
        cross_source, cross_target, small = sum_columns(
            contract_rows(weights_left, embed_source), contract_rows(weights_right, embed_target), small
        )
        if outer == 0:
            inverse_left = 1.0 / small[4]
            inverse_right = 1.0 / small[5]
            source_mass = mass_source * inverse_left[0]
            target_mass = mass_target * inverse_right[0]
            left = left * inverse_left[0]
            right = right * inverse_right[0]
        else:
            marg_left = small[1]
            marg_right = small[3]
            middle = jnp.cbrt(kernel_middle * scale_left * marg_left * scale_right * marg_right)
            inverse_left = middle / marg_left
            inverse_right = middle / marg_right
            left = weights_left * inverse_left[None, :]
            right = weights_right * inverse_right[None, :]
        cross_source = cross_source * inverse_left[:, None]
        cross_target = cross_target * inverse_right[:, None]
        heavy_source, plain_source = small[0] * inverse_left, small[1] * inverse_left
        heavy_target, plain_target = small[2] * inverse_right, small[3] * inverse_right
        diagonal = (
            heavy_source * plain_target + plain_source * heavy_target - 2.0 * jnp.sum(cross_source * cross_target, 1)
        )
        grad_middle = -diagonal / (middle * middle)
        over = 1.0 / middle
        grad_left = (
            norm_source[:, None] * (plain_target * over)[None, :]
            + (heavy_target * over)[None, :]
            - 2.0
            * lax.dot_general(
                embed_source, cross_target * over[:, None], (((1,), (1,)), ((), ())), precision=HIGH
            )
        )
        grad_right = (
            norm_target[:, None] * (plain_source * over)[None, :]
            + (heavy_source * over)[None, :]
            - 2.0
            * lax.dot_general(
                embed_target, cross_source * over[:, None], (((1,), (1,)), ((), ())), precision=HIGH
            )
        )
        peak = max_all(jnp.maximum(jnp.max(jnp.abs(grad_left)), jnp.max(jnp.abs(grad_right))))
        peak = jnp.maximum(peak, jnp.max(jnp.abs(grad_middle)))
        rate = 30.0 / (peak * peak + 1e-06)
        kernel_left = left * jnp.exp(-rate * grad_left)
        kernel_right = right * jnp.exp(-rate * grad_right)
        kernel_middle = middle * jnp.exp(-rate * grad_middle)
        scale_left = jnp.ones((rank,), jnp.float32)
        scale_right = jnp.ones((rank,), jnp.float32)
        for inner in range(INNER):
            row_left = source_mass / jnp.dot(kernel_left, scale_left, precision=HIGH)
            row_right = target_mass / jnp.dot(kernel_right, scale_right, precision=HIGH)
            if outer < OUTER - 1 and inner == INNER - 1:
                weights_left = row_left[:, None] * kernel_left
                weights_right = row_right[:, None] * kernel_right
                break
            margins = sum_all(
                jnp.stack(
                    [
                        jnp.dot(row_left, kernel_left, precision=HIGH),
                        jnp.dot(row_right, kernel_right, precision=HIGH),
                    ]
                )
            )
            marg_left = margins[0]
            marg_right = margins[1]
            middle = jnp.cbrt(kernel_middle * scale_left * marg_left * scale_right * marg_right)
            scale_left = middle / marg_left
            scale_right = middle / marg_right
    left = row_left[:, None] * kernel_left * scale_left[None, :]
    right = row_right[:, None] * kernel_right * scale_right[None, :]
    total_points = left.shape[0] * lax.axis_size(AXES)
    factor = float(total_points * rank)
    return (left * factor, right * factor, middle * float(rank))


def solution(mesh):
    mesh = Mesh(mesh.devices.reshape(4, 2, 8, 4), AXES)
    return jax.shard_map(
        local,
        mesh=mesh,
        in_specs=(
            P(AXES, None),
            P(AXES, None),
            P(AXES),
            P(AXES),
            P(AXES, None),
            P(AXES, None),
        ),
        out_specs=(P(AXES, None), P(AXES, None), P()),
        check_vma=False,
    )
```

```python
import jax
import jax.numpy as jnp
from jax import lax
from jax.experimental import pallas as pl
from jax.experimental.pallas import tpu as pltpu
from jax.sharding import Mesh, PartitionSpec as P

OUTER = 2
INNER = 8
LANES = 128
AXES = ("x", "core", "z", "y")
PLANE = ("x", "core", "y")
HIGH = lax.Precision.HIGHEST
F32 = jnp.float32


def chunks(n):
    return [slice(j, j + LANES) for j in range(0, n, LANES)]


def column(row):
    return jnp.transpose(jnp.broadcast_to(row, (LANES, row.shape[1])))


def row_of(partial):
    return jnp.sum(jnp.transpose(partial), 0, keepdims=True)


def widen(col, n):
    return jnp.concatenate([col] * (n // LANES), 1)


def pack(weights, embeds, norms, packed_ref, extra):
    rank, width = packed_ref.shape[0], embeds[0].shape[1]
    lane = lax.broadcasted_iota(jnp.int32, (rank, LANES), 1)
    small = jnp.zeros((rank, LANES), F32)
    for s in range(2):
        w = weights[s]
        packed_ref[:, s * width : (s + 1) * width] = jnp.dot(w, embeds[s], precision=HIGH, preferred_element_type=F32)
        small = jnp.where(lane == 2 * s, jnp.sum(w * norms[s], 1, keepdims=True), small)
        small = jnp.where(lane == 2 * s + 1, jnp.sum(w, 1, keepdims=True), small)
    for n, value in enumerate(extra):
        small = jnp.where(lane == 4 + n, value, small)
    packed_ref[:, 2 * width :] = small


def begin_kernel(x_ref, y_ref, a_ref, b_ref, mass_ref, w1_ref, w2_ref, norm_ref, packed_ref):
    embeds, weights, norms, totals = [], [], [], []
    for s, (e_ref, f_ref, w_ref) in enumerate(((x_ref, a_ref, w1_ref), (y_ref, b_ref, w2_ref))):
        factor = jnp.transpose(f_ref[...])
        mass = mass_ref[s : s + 1, :]
        w_ref[...] = factor * (mass / jnp.sum(factor, 0, keepdims=True))
        e = e_ref[...]
        ones = jnp.ones((8, e.shape[1]), F32)
        norm = lax.dot_general(ones, e * e, (((1,), (1,)), ((), ())), precision=HIGH, preferred_element_type=F32)[:1]
        norm_ref[s : s + 1, :] = norm
        embeds.append(e)
        weights.append(w_ref[...])
        norms.append(norm)
        totals.append(jnp.sum(mass, 1, keepdims=True))
    pack(weights, embeds, norms, packed_ref, totals)


def gradients(full_ref, embeds, norm_ref, inverse, middle, grad_refs, peak_ref):
    rank, width = full_ref.shape[0], embeds[0].shape[1]
    small = full_ref[:, 2 * width :]
    cross = [full_ref[:, s * width : (s + 1) * width] * widen(inverse[s], width) for s in range(2)]
    heavy = [small[:, 2 * s : 2 * s + 1] * inverse[s] for s in range(2)]
    plain = [small[:, 2 * s + 1 : 2 * s + 2] * inverse[s] for s in range(2)]
    diagonal = heavy[0] * plain[1] + plain[0] * heavy[1] - 2.0 * jnp.sum(cross[0] * cross[1], 1, keepdims=True)
    grad_middle = -diagonal / (middle * middle)
    over = 1.0 / middle
    peak = jnp.max(jnp.abs(grad_middle), 0, keepdims=True)
    for s in range(2):
        product = lax.dot_general(
            cross[1 - s] * widen(-2.0 * over, width),
            embeds[s],
            (((1,), (1,)), ((), ())),
            precision=HIGH,
            preferred_element_type=F32,
        )
        points = product.shape[1]
        norm = norm_ref[s : s + 1, :]
        grad = product + widen(plain[1 - s] * over, points) * norm + widen(heavy[1 - s] * over, points)
        grad_refs[s][...] = grad
        for c in chunks(points):
            peak = jnp.maximum(peak, jnp.max(jnp.abs(grad[:, c]), 0, keepdims=True))
    peak_ref[...] = jnp.broadcast_to(jnp.max(peak, 1, keepdims=True), peak_ref.shape)
    return grad_middle


def rows(columns):
    n = columns[0].shape[0]
    lane = lax.broadcasted_iota(jnp.int32, (n, LANES), 1)
    block = jnp.zeros((n, LANES), F32)
    for i, c in enumerate(columns):
        block = jnp.where(lane == i, c, block)
    return jnp.transpose(block)[:8]


def first_gradients_kernel(full_ref, x_ref, y_ref, norm_ref, mass_ref, g1_ref, g2_ref, peak_ref, rows_ref, share_ref):
    rank = full_ref.shape[0]
    width = x_ref.shape[1]
    inverse = [
        1.0 / jnp.broadcast_to(full_ref[:, 2 * width + 4 + s : 2 * width + 5 + s], (rank, LANES)) for s in range(2)
    ]
    for s in range(2):
        mass = mass_ref[s : s + 1, :]
        share_ref[s : s + 1, :] = mass * widen(inverse[s][:1], mass.shape[1])
    middle = jnp.full((rank, LANES), 1.0 / rank, F32)
    grad_middle = gradients(
        full_ref, (x_ref[...], y_ref[...]), norm_ref, inverse, middle, (g1_ref, g2_ref), peak_ref
    )
    rows_ref[...] = rows([middle, grad_middle, inverse[0], inverse[1]])


def next_gradients_kernel(full_ref, x_ref, y_ref, norm_ref, scale_ref, kmid_ref, g1_ref, g2_ref, peak_ref, rows_ref):
    rank = full_ref.shape[0]
    width = x_ref.shape[1]
    marg = [
        jnp.broadcast_to(full_ref[:, 2 * width + 2 * s + 1 : 2 * width + 2 * s + 2], (rank, LANES)) for s in range(2)
    ]
    scale = [column(scale_ref[s : s + 1, :]) for s in range(2)]
    cubed = column(kmid_ref[...]) * scale[0] * marg[0] * scale[1] * marg[1]
    middle = jnp.exp(jnp.log(cubed) * (1.0 / 3.0))
    inverse = [middle / marg[s] for s in range(2)]
    grad_middle = gradients(
        full_ref, (x_ref[...], y_ref[...]), norm_ref, inverse, middle, (g1_ref, g2_ref), peak_ref
    )
    rows_ref[...] = rows([middle, grad_middle, inverse[0], inverse[1]])


def scaling(k_ref, share, scale):
    partial = jnp.zeros((k_ref.shape[0], LANES), F32)
    factors = []
    for c in chunks(k_ref.shape[1]):
        k = k_ref[:, c]
        total = jnp.sum(k if scale is None else k * scale, 0, keepdims=True)
        factor = share[:, c] / total
        partial = partial + k * factor
        factors.append(factor)
    return jnp.concatenate(factors, 1), row_of(partial)


def first_step_kernel(g1_ref, g2_ref, w1_ref, w2_ref, peak_ref, rows_ref, share_ref, k1_ref, k2_ref, kmid_ref, sums_ref):
    middle, grad_middle = rows_ref[0:1, :], rows_ref[1:2, :]
    peak = jnp.max(peak_ref[...], 1, keepdims=True)
    rate = 30.0 / (peak * peak + 1e-06)
    kmid_ref[...] = middle * jnp.exp(-rate * grad_middle)
    for s, (g_ref, w_ref, k_ref) in enumerate(((g1_ref, w1_ref, k1_ref), (g2_ref, w2_ref, k2_ref))):
        inverse = column(rows_ref[2 + s : 3 + s, :])
        for c in chunks(k_ref.shape[1]):
            k_ref[:, c] = (w_ref[:, c] * inverse) * jnp.exp(-rate * g_ref[:, c])
        _, sums_ref[s : s + 1, :] = scaling(k_ref, share_ref[s : s + 1, :], None)


def step_kernel(k1_ref, k2_ref, share_ref, scale_ref, sums_ref, *factor_ref):
    for s, k_ref in enumerate((k1_ref, k2_ref)):
        factor, sums_ref[s : s + 1, :] = scaling(
            k_ref, share_ref[s : s + 1, :], column(scale_ref[s : s + 1, :])
        )
        for ref in factor_ref:
            ref[s : s + 1, :] = factor


def last_step_kernel(k1_ref, k2_ref, share_ref, scale_ref, x_ref, y_ref, norm_ref, w1_ref, w2_ref, packed_ref):
    for s, (k_ref, w_ref) in enumerate(((k1_ref, w1_ref), (k2_ref, w2_ref))):
        scale = column(scale_ref[s : s + 1, :])
        for c in chunks(k_ref.shape[1]):
            k = k_ref[:, c]
            w_ref[:, c] = k * (share_ref[s : s + 1, c] / jnp.sum(k * scale, 0, keepdims=True))
    norms = [norm_ref[s : s + 1, :] for s in range(2)]
    pack((w1_ref[...], w2_ref[...]), (x_ref[...], y_ref[...]), norms, packed_ref, [])


def end_kernel(total, k1_ref, k2_ref, factor_ref, scale_ref, o1_ref, o2_ref):
    for s, (k_ref, o_ref) in enumerate(((k1_ref, o1_ref), (k2_ref, o2_ref))):
        scale = column(scale_ref[s : s + 1, :])
        for c in chunks(k_ref.shape[1]):
            value = (k_ref[:, c] * factor_ref[s : s + 1, c]) * scale * total
            o_ref[c, :] = jnp.transpose(value)


def in_vmem(shape):
    return pltpu.VMEM(shape, F32)


def to_vmem(array):
    return pltpu.with_memory_space_constraint(array, pltpu.VMEM)


def call(kernel, outs, *args):
    return pl.pallas_call(
        kernel, out_shape=outs, compiler_params=pltpu.CompilerParams(vmem_limit_bytes=32 * 2**20)
    )(*[to_vmem(a) for a in args])


def exchange(value, axes):
    return lax.all_to_all(jnp.broadcast_to(value[None], (lax.axis_size(axes),) + value.shape), axes, 0, 0)


def sum_all(value):
    value = jnp.sum(exchange(value, ("x", "core")), 0)
    return jnp.sum(exchange(value, ("z", "y")), 0)


def sum_columns(packed):
    rank, total = packed.shape
    count = lax.axis_size(PLANE)
    part = jnp.sum(lax.all_to_all(packed.reshape(count, rank // count, total), PLANE, 0, 0), 0)
    part = jnp.sum(exchange(part, "z"), 0)
    return exchange(part, PLANE).reshape(rank, total)


def max_all(value):
    return jnp.max(exchange(value, AXES), 0)


def local(embed_source, embed_target, mass_source, mass_target, start_source, start_target):
    points, rank = start_source.shape
    width = embed_source.shape[1]
    embeds = (embed_source, embed_target)
    tall, line, top, pair = in_vmem((rank, points)), in_vmem((8, rank)), in_vmem((1, LANES)), in_vmem((2, points))
    sums_of, packed_of = in_vmem((2, rank)), in_vmem((rank, 2 * width + LANES))
    mass = jnp.stack([mass_source, mass_target])
    w1, w2, norm, packed = call(
        begin_kernel, [tall, tall, pair, packed_of], *embeds, start_source, start_target, mass
    )
    for outer in range(OUTER):
        full = sum_columns(packed)
        if outer == 0:
            g1, g2, peak, small, share = call(
                first_gradients_kernel, [tall, tall, top, line, pair], full, *embeds, norm, mass
            )
        else:
            g1, g2, peak, small = call(
                next_gradients_kernel, [tall, tall, top, line], full, *embeds, norm, scale, kmid
            )
        k1, k2, kmid, sums = call(
            first_step_kernel, [tall, tall, in_vmem((1, rank)), sums_of], g1, g2, w1, w2, max_all(peak), small, share
        )
        scale = jnp.ones((2, rank), F32)
        for inner in range(INNER):
            if inner == INNER - 1 and outer < OUTER - 1:
                w1, w2, packed = call(
                    last_step_kernel, [tall, tall, packed_of], k1, k2, share, scale, *embeds, norm
                )
                break
            if inner == INNER - 1:
                sums, factor = call(step_kernel, [sums_of, pair], k1, k2, share, scale)
            elif inner > 0:
                (sums,) = call(step_kernel, [sums_of], k1, k2, share, scale)
            margins = sum_all(sums)
            middle = jnp.cbrt(kmid * scale[:1] * margins[:1] * scale[1:] * margins[1:])
            scale = middle / margins
    total = float(points * lax.axis_size(AXES) * rank)
    result = jax.ShapeDtypeStruct((points, rank), F32)
    left, right = call(lambda *refs: end_kernel(total, *refs), [result, result], k1, k2, factor, scale)
    return left, right, middle[0] * float(rank)


def solution(mesh):
    mesh = Mesh(mesh.devices.reshape(4, 2, 8, 4), AXES)
    return jax.shard_map(
        local,
        mesh=mesh,
        in_specs=(P(AXES, None), P(AXES, None), P(AXES), P(AXES), P(AXES, None), P(AXES, None)),
        out_specs=(P(AXES, None), P(AXES, None), P()),
        check_vma=False,
    )
```

```python
import jax
import jax.numpy as jnp
from jax import lax
from jax.experimental import pallas as pl
from jax.experimental.pallas import tpu as pltpu
from jax.sharding import Mesh, PartitionSpec as P

OUTER = 2
INNER = 8
LANES = 128
VMEM = 8 * 2**20
AXES = ("x", "core", "z", "y")
PLANE = ("x", "core", "y")
HIGH = lax.Precision.HIGHEST
F32 = jnp.float32


def chunks(n):
    return [slice(j, j + LANES) for j in range(0, n, LANES)]


def column(row):
    return jnp.transpose(jnp.broadcast_to(row, (LANES, row.shape[1])))


def row_of(partial):
    return jnp.sum(jnp.transpose(partial), 0, keepdims=True)


def widen(col, n):
    return jnp.concatenate([col] * (n // LANES), 1)


def pack(weights, embeds, norms, packed_ref, extra):
    rank, width = packed_ref.shape[0], embeds[0].shape[1]
    lane = lax.broadcasted_iota(jnp.int32, (rank, LANES), 1)
    small = jnp.zeros((rank, LANES), F32)
    for s in range(2):
        w = weights[s]
        packed_ref[:, s * width : (s + 1) * width] = jnp.dot(w, embeds[s], precision=HIGH, preferred_element_type=F32)
        small = jnp.where(lane == 2 * s, jnp.sum(w * norms[s], 1, keepdims=True), small)
        small = jnp.where(lane == 2 * s + 1, jnp.sum(w, 1, keepdims=True), small)
    for n, value in enumerate(extra):
        small = jnp.where(lane == 4 + n, value, small)
    packed_ref[:, 2 * width :] = small


def begin_kernel(x_ref, y_ref, a_ref, b_ref, m1_ref, m2_ref, w1_ref, w2_ref, norm_ref, packed_ref):
    embeds, weights, norms, totals = [], [], [], []
    for s, (e_ref, f_ref, m_ref, w_ref) in enumerate(
        ((x_ref, a_ref, m1_ref, w1_ref), (y_ref, b_ref, m2_ref, w2_ref))
    ):
        factor = jnp.transpose(f_ref[...])
        mass = m_ref[...]
        w_ref[...] = factor * (mass / jnp.sum(factor, 0, keepdims=True))
        e = e_ref[...]
        ones = jnp.ones((8, e.shape[1]), F32)
        norm = lax.dot_general(ones, e * e, (((1,), (1,)), ((), ())), precision=HIGH, preferred_element_type=F32)[:1]
        norm_ref[s : s + 1, :] = norm
        embeds.append(e)
        weights.append(w_ref[...])
        norms.append(norm)
        totals.append(jnp.sum(mass, 1, keepdims=True))
    pack(weights, embeds, norms, packed_ref, totals)


def fold_kernel(in_ref, out_ref):
    out_ref[...] = jnp.broadcast_to(jnp.sum(in_ref[...], 0, keepdims=True), out_ref.shape)


def add_kernel(a_ref, b_ref, out_ref):
    out_ref[...] = jnp.broadcast_to((a_ref[...] + b_ref[...])[None], out_ref.shape)


def summed(full_ref, inverse, middle):
    rank = full_ref.shape[0]
    width = (full_ref.shape[1] - LANES) // 2
    small = full_ref[:, 2 * width :]
    cross = [full_ref[:, s * width : (s + 1) * width] * widen(inverse[s], width) for s in range(2)]
    heavy = [small[:, 2 * s : 2 * s + 1] * inverse[s] for s in range(2)]
    plain = [small[:, 2 * s + 1 : 2 * s + 2] * inverse[s] for s in range(2)]
    diagonal = heavy[0] * plain[1] + plain[0] * heavy[1] - 2.0 * jnp.sum(cross[0] * cross[1], 1, keepdims=True)
    return cross, heavy, plain, 1.0 / middle, -diagonal / (middle * middle)


def gradient(terms, s, embed, norm, grad_ref, peak):
    cross, heavy, plain, over, _ = terms
    width = embed.shape[1]
    product = lax.dot_general(
        cross[1 - s] * widen(-2.0 * over, width),
        embed,
        (((1,), (1,)), ((), ())),
        precision=HIGH,
        preferred_element_type=F32,
    )
    points = product.shape[1]
    grad = product + widen(plain[1 - s] * over, points) * norm + widen(heavy[1 - s] * over, points)
    grad_ref[...] = grad
    for c in chunks(points):
        peak = jnp.maximum(peak, jnp.max(jnp.abs(grad[:, c]), 0, keepdims=True))
    return peak


def rows(columns):
    n = columns[0].shape[0]
    lane = lax.broadcasted_iota(jnp.int32, (n, LANES), 1)
    block = jnp.zeros((n, LANES), F32)
    for i, c in enumerate(columns):
        block = jnp.where(lane == i, c, block)
    return jnp.transpose(block)[:8]


def first_gradients_kernel(
    full_ref, x_ref, y_ref, norm_ref, m1_ref, m2_ref, g1_ref, g2_ref, peak_ref, rows_ref, share_ref
):
    rank, width = full_ref.shape[0], x_ref.shape[1]
    inverse = [
        1.0 / jnp.broadcast_to(full_ref[:, 2 * width + 4 + s : 2 * width + 5 + s], (rank, LANES)) for s in range(2)
    ]
    middle = jnp.full((rank, LANES), 1.0 / rank, F32)
    terms = summed(full_ref, inverse, middle)
    peak = jnp.max(jnp.abs(terms[-1]), 0, keepdims=True)
    for s, (e_ref, m_ref, g_ref) in enumerate(((x_ref, m1_ref, g1_ref), (y_ref, m2_ref, g2_ref))):
        mass = m_ref[...]
        share_ref[s : s + 1, :] = mass * widen(inverse[s][:1], mass.shape[1])
        peak = gradient(terms, s, e_ref[...], norm_ref[s : s + 1, :], g_ref, peak)
    peak_ref[...] = jnp.broadcast_to(peak[None], peak_ref.shape)
    rows_ref[...] = rows([middle, terms[-1], inverse[0], inverse[1]])


def next_gradients_kernel(full_ref, scale_ref, kmid_ref, *refs):
    e_refs, k_refs, (g1_ref, g2_ref, peak_ref, rows_ref) = refs[:8], refs[8:16], refs[16:]
    rank, width = full_ref.shape[0], e_refs[0].shape[1]
    marg = [
        jnp.broadcast_to(full_ref[:, 2 * width + 2 * s + 1 : 2 * width + 2 * s + 2], (rank, LANES)) for s in range(2)
    ]
    scale = [column(scale_ref[s : s + 1, :]) for s in range(2)]
    middle = cube_root(column(kmid_ref[...]) * scale[0] * marg[0] * scale[1] * marg[1])
    inverse = [middle / marg[s] for s in range(2)]
    terms = summed(full_ref, inverse, middle)
    peak = jnp.max(jnp.abs(terms[-1]), 0, keepdims=True)
    for s, g_ref in enumerate((g1_ref, g2_ref)):
        for j in range(4):
            norm = k_refs[4 * s + j][rank + 1 : rank + 2, :]
            peak = gradient(terms, s, e_refs[4 * s + j][...], norm, g_ref.at[j], peak)
    peak_ref[...] = jnp.broadcast_to(peak[None], peak_ref.shape)
    rows_ref[...] = rows([middle, terms[-1], inverse[0], inverse[1]])


def cube_root(value):
    return jnp.exp(jnp.log(value) * (1.0 / 3.0))


def rescale(margins_ref, kmid_ref, scale_ref):
    margins = jnp.sum(margins_ref[...], 0)
    first, second = margins[0:1], margins[1:2]
    if scale_ref is None:
        middle = cube_root(kmid_ref[...] * first * second)
    else:
        middle = cube_root(kmid_ref[...] * scale_ref[0:1, :] * first * scale_ref[1:2, :] * second)
    return middle, [middle / first, middle / second]


def row_factor(k, share, scale):
    return share / jnp.sum(k if scale is None else k * scale, 0, keepdims=True)


def scaling(k_refs, rank, scale, factor_refs):
    partials = []
    for k_ref in k_refs:
        partial = jnp.zeros((rank, LANES), F32)
        for c in chunks(k_ref.shape[1]):
            k = k_ref[:rank, c]
            factor = row_factor(k, k_ref[rank : rank + 1, c], scale)
            partial = partial + k * factor
            if k_ref is k_refs[0]:
                for ref in factor_refs:
                    ref[:, c] = factor
        partials.append(partial)
    return row_of(partials[0] if len(partials) == 1 else (partials[0] + partials[1]) + (partials[2] + partials[3]))


def put(sums_ref, s, row):
    if len(sums_ref.shape) == 2:
        sums_ref[s : s + 1, :] = row
    else:
        sums_ref[:, s : s + 1, :] = jnp.broadcast_to(row[None], (sums_ref.shape[0],) + row.shape)


def rate_of(peak_ref):
    peak = jnp.max(jnp.max(peak_ref[...], 0), 1, keepdims=True)
    return 30.0 / (peak * peak + 1e-06)


def first_step_kernel(
    g1_ref, g2_ref, w1_ref, w2_ref, peak_ref, rows_ref, share_ref, norm_ref, k1_ref, k2_ref, kmid_ref, sums_ref
):
    rank = w1_ref.shape[0]
    rate = rate_of(peak_ref)
    kmid_ref[...] = rows_ref[0:1, :] * jnp.exp(-rate * rows_ref[1:2, :])
    for s, (g_ref, w_ref, k_ref) in enumerate(((g1_ref, w1_ref, k1_ref), (g2_ref, w2_ref, k2_ref))):
        inverse = column(rows_ref[2 + s : 3 + s, :])
        for c in chunks(k_ref.shape[1]):
            k_ref[:rank, c] = (w_ref[:, c] * inverse) * jnp.exp(-rate * g_ref[:, c])
        k_ref[rank : rank + 1, :] = share_ref[s : s + 1, :]
        k_ref[rank + 1 : rank + 2, :] = norm_ref[s : s + 1, :]
        k_ref[rank + 2 :, :] = jnp.zeros((k_ref.shape[0] - rank - 2, k_ref.shape[1]), F32)
        put(sums_ref, s, scaling([k_ref], rank, None, ()))


def next_first_step_kernel(g1_ref, g2_ref, peak_ref, rows_ref, factor_ref, *refs):
    old_refs, new_refs, (kmid_ref, sums_ref) = refs[:8], refs[8:16], refs[16:]
    rank = g1_ref.shape[1]
    rate = rate_of(peak_ref)
    kmid_ref[...] = rows_ref[0:1, :] * jnp.exp(-rate * rows_ref[1:2, :])
    for s, g_ref in enumerate((g1_ref, g2_ref)):
        inverse = column(rows_ref[2 + s : 3 + s, :])
        for j in range(4):
            old_ref, new_ref = old_refs[4 * s + j], new_refs[4 * s + j]
            factor = factor_ref[4 * s + j : 4 * s + j + 1, :]
            for c in chunks(old_ref.shape[1]):
                new_ref[:rank, c] = (old_ref[:rank, c] * factor[:, c] * inverse) * jnp.exp(-rate * g_ref[j, :, c])
            new_ref[rank:, :] = old_ref[rank:, :]
        put(sums_ref, s, scaling(new_refs[4 * s : 4 * s + 4], rank, None, ()))


def step_kernel(n, initial, margins_ref, kmid_ref, *refs):
    scale_ref, refs = (None, refs) if initial else (refs[0], refs[1:])
    k_refs, sums_ref, new_ref, factor_refs = refs[: 2 * n], refs[2 * n], refs[2 * n + 1], refs[2 * n + 2 :]
    rank = kmid_ref.shape[1]
    _, scales = rescale(margins_ref, kmid_ref, scale_ref)
    for s in range(2):
        new_ref[s : s + 1, :] = scales[s]
        part = [ref.at[s : s + 1, :] for ref in factor_refs]
        put(sums_ref, s, scaling(k_refs[n * s : n * s + n], rank, column(scales[s]), part))


def last_step_kernel(margins_ref, kmid_ref, scale_ref, x_ref, y_ref, *refs):
    k_refs, (factor_ref, new_ref, packed_ref) = refs[:8], refs[8:]
    rank = kmid_ref.shape[1]
    weights, norms = [], []
    _, scales = rescale(margins_ref, kmid_ref, scale_ref)
    for s in range(2):
        new_ref[s : s + 1, :] = scales[s]
        scale = column(scales[s])
        for j in range(4):
            k_ref = k_refs[4 * s + j]
            for c in chunks(k_ref.shape[1]):
                factor_ref[4 * s + j : 4 * s + j + 1, c] = row_factor(
                    k_ref[:rank, c], k_ref[rank : rank + 1, c], scale
                )
        weights.append(k_refs[4 * s][:rank, :] * factor_ref[4 * s : 4 * s + 1, :])
        norms.append(k_refs[4 * s][rank + 1 : rank + 2, :])
    pack(weights, (x_ref[...], y_ref[...]), norms, packed_ref, [])


def end_kernel(total, margins_ref, kmid_ref, scale_ref, k1_ref, k2_ref, factor_ref, o1_ref, o2_ref, middle_ref):
    rank = kmid_ref.shape[1]
    middle, scales = rescale(margins_ref, kmid_ref, scale_ref)
    middle_ref[...] = middle * float(rank)
    for s, (k_ref, o_ref) in enumerate(((k1_ref, o1_ref), (k2_ref, o2_ref))):
        scale = column(scales[s])
        for c in chunks(k_ref.shape[1]):
            value = (k_ref[:rank, c] * factor_ref[s : s + 1, c]) * scale * total
            o_ref[c, :] = jnp.transpose(value)


def in_vmem(*shape):
    return pltpu.VMEM(shape, F32)


def to_vmem(array):
    return pltpu.with_memory_space_constraint(array, pltpu.VMEM)


def call(kernel, outs, *args):
    return pl.pallas_call(
        kernel, out_shape=outs, compiler_params=pltpu.CompilerParams(vmem_limit_bytes=VMEM)
    )(*[to_vmem(a) for a in args])


def across(value, bits):
    return lax.ppermute(value, "x", [(i, i ^ bits) for i in range(lax.axis_size("x"))])


def swap(value, axes):
    return lax.all_to_all(value, axes, 0, 0)


def beside(value, sends):
    if not sends:
        return swap(value, ("z", "y")), []
    blocks, value = lax.optimization_barrier(([block for block, _ in sends], value))
    got = [across(block, bits) for block, (_, bits) in zip(blocks, sends)]
    return lax.optimization_barrier((swap(value, ("z", "y")), got))


def sum_all(value, sends):
    value = swap(value, ("x", "core"))
    (value,) = call(fold_kernel, [in_vmem(lax.axis_size(("z", "y")), *value.shape[1:])], value)
    return beside(value, sends)


def sum_rest(value, sends):
    other = lax.ppermute(value, "core", [(0, 1), (1, 0)])
    (value,) = call(add_kernel, [in_vmem(lax.axis_size(("z", "y")), *value.shape)], value, other)
    return beside(value, sends)


def sum_columns(packed):
    rank, total = packed.shape
    count, deep = lax.axis_size(PLANE), lax.axis_size("z")
    part = swap(packed.reshape(count, rank // count, total), PLANE)
    (part,) = call(fold_kernel, [in_vmem(deep, rank // count, total)], part)
    (part,) = call(fold_kernel, [in_vmem(count, rank // count, total)], swap(part, "z"))
    return swap(part, PLANE).reshape(rank, total)


def local(embed_source, embed_target, mass_source, mass_target, start_source, start_target):
    points, rank = start_source.shape
    width = embed_source.shape[1]
    embeds, masses = (embed_source, embed_target), (mass_source[None], mass_target[None])
    tall, line, pair = in_vmem(rank, points), in_vmem(8, rank), in_vmem(2, points)
    sums_of, packed_of, mid_of = in_vmem(2, rank), in_vmem(rank, 2 * width + LANES), in_vmem(1, rank)
    sums_in = in_vmem(lax.axis_size(("x", "core")), 2, rank)
    block, four = in_vmem(rank + 8, points), in_vmem(4, rank, points)
    part = ("core", "z", "y")
    w1, w2, norm, packed = call(
        begin_kernel, [tall, tall, pair, packed_of], *embeds, start_source, start_target, *masses
    )
    full = sum_columns(packed)
    g1, g2, peak, small, share = call(
        first_gradients_kernel,
        [tall, tall, in_vmem(lax.axis_size(AXES), 1, LANES), line, pair],
        full,
        *embeds,
        norm,
        *masses,
    )
    k1, k2, kmid, sums = call(
        first_step_kernel, [block, block, mid_of, sums_in], g1, g2, w1, w2, swap(peak, AXES), small, share, norm
    )
    margins, (k1_1, k2_3) = sum_all(sums, [(k1, 1), (k2, 3)])
    sums, scale = call(
        lambda *refs: step_kernel(1, True, *refs), [sums_in, sums_of], margins, kmid, k1, k2
    )
    margins, (k1_2, k2_2) = sum_all(sums, [(k1_1, 3), (k2_3, 1)])
    sums, scale = call(
        lambda *refs: step_kernel(1, False, *refs), [sums_in, sums_of], margins, kmid, scale, k1, k2
    )
    margins, (k1_3, k2_1) = sum_all(sums, [(k1, 3), (k2, 1)])
    blocks = (k1, k1_1, k1_3, k1_2, k2, k2_1, k2_3, k2_2)
    step = lambda *refs: step_kernel(4, False, *refs)
    for inner in range(3, INNER - 1):
        sums, scale = call(step, [sums_of, sums_of], margins, kmid, scale, *blocks)
        if inner == 3:
            margins, (x_1, y_3) = sum_rest(sums, [(embed_source, 1), (embed_target, 3)])
        elif inner == 4:
            margins, (x_2, y_2) = sum_rest(sums, [(x_1, 3), (y_3, 1)])
        elif inner == 5:
            margins, (x_3, y_1) = sum_rest(sums, [(embed_source, 3), (embed_target, 1)])
        else:
            margins, _ = sum_rest(sums, [])
    near = (embed_source, x_1, x_3, x_2, embed_target, y_1, y_3, y_2)
    for outer in range(1, OUTER):
        factor, scale, packed = call(
            last_step_kernel, [in_vmem(8, points), sums_of, packed_of], margins, kmid, scale, *embeds, *blocks
        )
        full = sum_columns(packed)
        g1, g2, peak, small = call(
            next_gradients_kernel,
            [four, four, in_vmem(lax.axis_size(part), 1, LANES), line],
            full,
            scale,
            kmid,
            *near,
            *blocks,
        )
        *blocks, kmid, sums = call(
            next_first_step_kernel, [block] * 8 + [mid_of, sums_of], g1, g2, swap(peak, part), small, factor, *blocks
        )
        margins, _ = sum_rest(sums, [])
        for inner in range(1, INNER - 1):
            initial = inner == 1
            before = () if initial else (scale,)
            sums, scale = call(
                lambda *refs: step_kernel(4, initial, *refs), [sums_of, sums_of], margins, kmid, *before, *blocks
            )
            margins, _ = sum_rest(sums, [])
    sums, scale, factor = call(step, [sums_of, sums_of, pair], margins, kmid, scale, *blocks)
    margins, _ = sum_rest(sums, [])
    total = float(points * lax.axis_size(AXES) * rank)
    result = jax.ShapeDtypeStruct((points, rank), F32)
    left, right, middle = call(
        lambda *refs: end_kernel(total, *refs),
        [result, result, jax.ShapeDtypeStruct((1, rank), F32)],
        margins,
        kmid,
        scale,
        blocks[0],
        blocks[4],
        factor,
    )
    return left, right, middle[0]


def solution(mesh):
    mesh = Mesh(mesh.devices.reshape(4, 2, 8, 4), AXES)
    return jax.shard_map(
        local,
        mesh=mesh,
        in_specs=(P(AXES, None), P(AXES, None), P(AXES), P(AXES), P(AXES, None), P(AXES, None)),
        out_specs=(P(AXES, None), P(AXES, None), P()),
        check_vma=False,
    )
```

```python
import jax
import jax.numpy as jnp
from jax import lax
from jax.experimental import pallas as pl
from jax.experimental.pallas import tpu as pltpu
from jax.sharding import Mesh, PartitionSpec as P

OUTER = 2
INNER = 8
LANES = 128
VMEM = 8 * 2**20
AXES = ("x", "core", "z", "y")
HIGH = lax.Precision.HIGHEST
F32 = jnp.float32


def chunks(n):
    return [slice(j, j + LANES) for j in range(0, n, LANES)]


def column(row):
    return jnp.transpose(jnp.broadcast_to(row, (LANES, row.shape[1])))


def row_of(partial):
    return jnp.sum(jnp.transpose(partial), 0, keepdims=True)


def widen(col, n):
    return jnp.concatenate([col] * (n // LANES), 1)


def pack(weights, embeds, norms, packed_ref, extra):
    rank, width = packed_ref.shape[0], embeds[0][0].shape[1]
    lane = lax.broadcasted_iota(jnp.int32, (rank, LANES), 1)
    small = jnp.zeros((rank, LANES), F32)
    for s in range(2):
        product = heavy = plain = 0.0
        for w, e, n in zip(weights, embeds, norms):
            product = product + jnp.dot(w[s], e[s], precision=HIGH, preferred_element_type=F32)
            heavy = heavy + jnp.sum(w[s] * n[s], 1, keepdims=True)
            plain = plain + jnp.sum(w[s], 1, keepdims=True)
        packed_ref[:, s * width : (s + 1) * width] = product
        small = jnp.where(lane == 2 * s, heavy, small)
        small = jnp.where(lane == 2 * s + 1, plain, small)
    for n, value in enumerate(extra):
        small = jnp.where(lane == 4 + n, value, small)
    packed_ref[:, 2 * width :] = small


def norms_of(embed):
    ones = jnp.ones((8, embed.shape[1]), F32)
    square = embed * embed
    return lax.dot_general(ones, square, (((1,), (1,)), ((), ())), precision=HIGH, preferred_element_type=F32)[:1]


def halves(ref):
    half = ref.shape[0] // 2
    core = lax.axis_index("core")
    return [pl.ds(pl.multiple_of(c * half, 8), half) for c in (core, 1 - core)]


def begin_kernel(
    x_in,
    y_in,
    a_in,
    b_in,
    m1_in,
    m2_in,
    x_ref,
    y_ref,
    w1_ref,
    w2_ref,
    keep_ref,
    send_ref,
    packed_ref,
    a_ref,
    b_ref,
    m1_ref,
    m2_ref,
    sems,
):
    pairs = ((m1_in, m1_ref), (m2_in, m2_ref), (a_in, a_ref), (x_in, x_ref), (b_in, b_ref), (y_in, y_ref))
    copies = [pltpu.make_async_copy(source, target, sems.at[n]) for n, (source, target) in enumerate(pairs)]
    for copy in copies:
        copy.start()
    for copy in copies:
        copy.wait()
    embeds, weights, norms, totals = [], [], [], []
    for e_ref, f_ref, m_ref, w_ref in ((x_ref, a_ref, m1_ref, w1_ref), (y_ref, b_ref, m2_ref, w2_ref)):
        factor = jnp.transpose(f_ref[...])
        rank = factor.shape[0]
        mass = m_ref[...]
        weight = factor * (mass / jnp.sum(factor, 0, keepdims=True))
        embeds.append(e_ref[...])
        weights.append(weight)
        norms.append(norms_of(embeds[-1]))
        totals.append(jnp.sum(mass, 1, keepdims=True))
        w_ref[:rank, :] = weight
        w_ref[rank : rank + 1, :] = mass
        w_ref[rank + 1 :, :] = jnp.broadcast_to(norms[-1], (w_ref.shape[0] - rank - 1, mass.shape[1]))
    pack([weights], [embeds], [norms], packed_ref, totals)
    mine, others = halves(packed_ref)
    keep_ref[...] = packed_ref[mine, :]
    send_ref[...] = packed_ref[others, :]


def fold_kernel(in_ref, out_ref):
    out_ref[...] = jnp.broadcast_to(jnp.sum(in_ref[...], 0, keepdims=True), out_ref.shape)


def add_kernel(a_ref, b_ref, out_ref):
    value = a_ref[...] + b_ref[...]
    out_ref[...] = value if value.shape == out_ref.shape else jnp.broadcast_to(value[None], out_ref.shape)


def summed(full_ref, inverse, middle):
    rank = full_ref.shape[0]
    width = (full_ref.shape[1] - LANES) // 2
    small = full_ref[:, 2 * width :]
    cross = [full_ref[:, s * width : (s + 1) * width] * widen(inverse[s], width) for s in range(2)]
    heavy = [small[:, 2 * s : 2 * s + 1] * inverse[s] for s in range(2)]
    plain = [small[:, 2 * s + 1 : 2 * s + 2] * inverse[s] for s in range(2)]
    diagonal = heavy[0] * plain[1] + plain[0] * heavy[1] - 2.0 * jnp.sum(cross[0] * cross[1], 1, keepdims=True)
    return cross, heavy, plain, 1.0 / middle, -diagonal / (middle * middle)


def gradient(terms, s, embed, norm, grad_ref, peak):
    cross, heavy, plain, over, _ = terms
    width = embed.shape[1]
    product = lax.dot_general(
        cross[1 - s] * widen(-2.0 * over, width),
        embed,
        (((1,), (1,)), ((), ())),
        precision=HIGH,
        preferred_element_type=F32,
    )
    points = product.shape[1]
    grad = product + widen(plain[1 - s] * over, points) * norm + widen(heavy[1 - s] * over, points)
    grad_ref[...] = grad
    for c in chunks(points):
        peak = jnp.maximum(peak, jnp.max(jnp.abs(grad[:, c]), 0, keepdims=True))
    return peak


def rows(columns):
    n = columns[0].shape[0]
    lane = lax.broadcasted_iota(jnp.int32, (n, LANES), 1)
    block = jnp.zeros((n, LANES), F32)
    for i, c in enumerate(columns):
        block = jnp.where(lane == i, c, block)
    return jnp.transpose(block)[:8]


def gradients_kernel(first, n, own_ref, other_ref, *refs):
    before, refs = ((), refs) if first else (refs[:2], refs[2:])
    e_refs, k_refs = refs[: 2 * n], refs[2 * n : 4 * n]
    g1_ref, g2_ref, peak_ref, rows_ref, full_ref = refs[4 * n :]
    rank, width = full_ref.shape[0], e_refs[0].shape[1]
    mine, others = halves(full_ref)
    full_ref[mine, :] = own_ref[...]
    full_ref[others, :] = other_ref[...]

    def small(i):
        return jnp.broadcast_to(full_ref[:, 2 * width + i : 2 * width + i + 1], (rank, LANES))

    if first:
        inverse = [1.0 / small(4), 1.0 / small(5)]
        middle = jnp.full((rank, LANES), 1.0 / rank, F32)
    else:
        scale_ref, kmid_ref = before
        marg = [small(1), small(3)]
        scale = [column(scale_ref[s : s + 1, :]) for s in range(2)]
        middle = cube_root(column(kmid_ref[...]) * scale[0] * marg[0] * scale[1] * marg[1])
        inverse = [middle / marg[s] for s in range(2)]
    terms = summed(full_ref, inverse, middle)
    peak = jnp.max(jnp.abs(terms[-1]), 0, keepdims=True)
    for s, g_ref in enumerate((g1_ref, g2_ref)):
        for j in range(n):
            norm = k_refs[n * s + j][rank + 1 : rank + 2, :]
            peak = gradient(terms, s, e_refs[n * s + j][...], norm, g_ref.at[j], peak)
    peak_ref[...] = jnp.broadcast_to(peak[None], peak_ref.shape)
    rows_ref[...] = rows([middle, terms[-1], inverse[0], inverse[1]])


def cube_root(value):
    return jnp.exp(jnp.log(value) * (1.0 / 3.0))


def rescale(margins_ref, kmid_ref, scale_ref):
    margins = jnp.sum(margins_ref[...], 0)
    first, second = margins[0:1], margins[1:2]
    if scale_ref is None:
        middle = cube_root(kmid_ref[...] * first * second)
    else:
        middle = cube_root(kmid_ref[...] * scale_ref[0:1, :] * first * scale_ref[1:2, :] * second)
    return middle, [middle / first, middle / second]


def scaling(k_refs, rank, scale):
    groups = [slice(i, i + 8) for i in range(0, rank, 8)]
    points = k_refs[0].shape[1]
    totals = [jnp.zeros((8, points), F32) for _ in k_refs]
    for i in groups:
        wide = None if scale is None else widen(scale[i], points)
        for j, k_ref in enumerate(k_refs):
            totals[j] = totals[j] + (k_ref[i, :] if scale is None else k_ref[i, :] * wide)
    factors = [
        k_ref[rank : rank + 1, :] / jnp.sum(total, 0, keepdims=True) for k_ref, total in zip(k_refs, totals)
    ]
    wides = [jnp.broadcast_to(factor, (8, points)) for factor in factors]
    partials = []
    for i in groups:
        parts = []
        for k_ref, wide in zip(k_refs, wides):
            product = k_ref[i, :] * wide
            part = product[:, :LANES]
            for c in chunks(points)[1:]:
                part = part + product[:, c]
            parts.append(part)
        partials.append(parts[0] if len(parts) == 1 else (parts[0] + parts[1]) + (parts[2] + parts[3]))
    return factors, row_of(jnp.concatenate(partials, 0))


def rate_of(peak_ref):
    peak = jnp.max(jnp.max(peak_ref[...], 0), 1, keepdims=True)
    return 30.0 / (peak * peak + 1e-06)


def first_step_kernel(first, n, g1_ref, g2_ref, peak_ref, rows_ref, *refs):
    factors, refs = ((), refs) if first else (refs[:1], refs[1:])
    old_refs, new_refs, (kmid_ref, sums_ref) = refs[: 2 * n], refs[2 * n : 4 * n], refs[4 * n :]
    rank = g1_ref.shape[1]
    rate = rate_of(peak_ref)
    kmid_ref[...] = rows_ref[0:1, :] * jnp.exp(-rate * rows_ref[1:2, :])
    for s, g_ref in enumerate((g1_ref, g2_ref)):
        inverse = column(rows_ref[2 + s : 3 + s, :])
        for j in range(n):
            b = n * s + j
            old_ref, new_ref = old_refs[b], new_refs[b]
            for c in chunks(old_ref.shape[1]):
                old = old_ref[:rank, c]
                for ref in factors:
                    old = old * ref[b : b + 1, c]
                new_ref[:rank, c] = (old * inverse) * jnp.exp(-rate * g_ref[j, :, c])
            new_ref[rank:, :] = old_ref[rank:, :]
            if first:
                new_ref[rank : rank + 1, :] = old_ref[rank : rank + 1, :] * rows_ref[2 + s : 3 + s, 0:1]
        _, row = scaling(new_refs[n * s : n * s + n], rank, None)
        put(sums_ref, s, row)


def step_kernel(initial, n, margins_ref, kmid_ref, *refs):
    scale_ref, refs = (None, refs) if initial else (refs[0], refs[1:])
    k_refs, sums_ref, new_ref, factor_refs = refs[: 2 * n], refs[2 * n], refs[2 * n + 1], refs[2 * n + 2 :]
    rank = kmid_ref.shape[1]
    _, scales = rescale(margins_ref, kmid_ref, scale_ref)
    for s in range(2):
        new_ref[s : s + 1, :] = scales[s]
        factors, row = scaling(k_refs[n * s : n * s + n], rank, column(scales[s]))
        put(sums_ref, s, row)
        for ref in factor_refs:
            ref[s : s + 1, :] = factors[0]


def put(sums_ref, s, row):
    if len(sums_ref.shape) == 2:
        sums_ref[s : s + 1, :] = row
    else:
        sums_ref[:, s : s + 1, :] = jnp.broadcast_to(row[None], (sums_ref.shape[0],) + row.shape)


def last_step_kernel(margins_ref, kmid_ref, scale_ref, *refs):
    e_refs, k_refs, (factor_ref, new_ref, packed_ref) = refs[:8], refs[8:16], refs[16:]
    rank, part = kmid_ref.shape[1], packed_ref.shape[0] // 2
    ours = [pl.ds(pl.multiple_of(c * (rank // 2) + lax.axis_index("x") * part, 8), part) for c in range(2)]
    weights = [[None, None] for _ in range(4)]
    norms = [[None, None] for _ in range(4)]
    _, scales = rescale(margins_ref, kmid_ref, scale_ref)
    for s in range(2):
        new_ref[s : s + 1, :] = scales[s]
        scale = column(scales[s])
        for j in range(4):
            n = 4 * s + j
            k_ref = k_refs[n]
            for c in chunks(k_ref.shape[1]):
                total = jnp.sum(k_ref[:rank, c] * scale, 0, keepdims=True)
                factor_ref[n : n + 1, c] = k_ref[rank : rank + 1, c] / total
            weights[j][s] = jnp.concatenate([k_ref[o, :] for o in ours], 0) * factor_ref[n : n + 1, :]
            norms[j][s] = k_ref[rank + 1 : rank + 2, :]
    embeds = [(e_refs[j][...], e_refs[4 + j][...]) for j in range(4)]
    pack(weights, embeds, norms, packed_ref, [])


def end_kernel(total, margins_ref, kmid_ref, scale_ref, k1_ref, k2_ref, factor_ref, o1_ref, o2_ref, middle_ref):
    rank = kmid_ref.shape[1]
    middle, scales = rescale(margins_ref, kmid_ref, scale_ref)
    middle_ref[...] = middle * float(rank)
    for s, (k_ref, o_ref) in enumerate(((k1_ref, o1_ref), (k2_ref, o2_ref))):
        scale = column(scales[s])
        for c in chunks(k_ref.shape[1]):
            value = (k_ref[:rank, c] * factor_ref[s : s + 1, c]) * scale * total
            o_ref[c, :] = jnp.transpose(value)


def in_vmem(*shape):
    return pltpu.VMEM(shape, F32)


def to_vmem(array):
    return pltpu.with_memory_space_constraint(array, pltpu.VMEM)


def call(kernel, outs, *args, scratch=()):
    return pl.pallas_call(
        kernel,
        out_shape=outs,
        scratch_shapes=[pltpu.VMEM(shape, F32) for shape in scratch],
        compiler_params=pltpu.CompilerParams(vmem_limit_bytes=VMEM),
    )(*[to_vmem(a) for a in args])


def across(value, bits):
    return lax.ppermute(value, "x", [(i, i ^ bits) for i in range(lax.axis_size("x"))])


def swap(value, axes):
    return lax.all_to_all(value, axes, 0, 0)


def beside(value, axes, sends):
    if not sends:
        return swap(value, axes), []
    blocks, value = lax.optimization_barrier(([block for block, _ in sends], value))
    got = [across(block, bits) for block, (_, bits) in zip(blocks, sends)]
    return lax.optimization_barrier((swap(value, axes), got))


def sum_all(value, sends):
    value = swap(value, ("x", "core"))
    (value,) = call(fold_kernel, [in_vmem(lax.axis_size(("z", "y")), *value.shape[1:])], value)
    return beside(value, ("z", "y"), sends)


def other_core(value):
    return lax.ppermute(value, "core", [(0, 1), (1, 0)])


def sum_rest(value, sends=()):
    (value,) = call(add_kernel, [in_vmem(lax.axis_size(("z", "y")), *value.shape)], value, other_core(value))
    return beside(value, ("z", "y"), sends)


def sum_along(part, axes):
    deep, wide, shape = lax.axis_size("z"), lax.axis_size(("x", "y")), part.shape[1:]
    (part,) = call(fold_kernel, [in_vmem(deep, *shape)], swap(part, axes))
    (part,) = call(fold_kernel, [in_vmem(wide, *shape)], swap(part, "z"))
    own = swap(part, ("x", "y")).reshape(wide * shape[0], shape[1])
    return own, other_core(own)


def sum_columns(keep, send):
    (part,) = call(add_kernel, [in_vmem(*keep.shape)], keep, other_core(send))
    count = lax.axis_size(("x", "y"))
    return sum_along(part.reshape(count, keep.shape[0] // count, keep.shape[1]), ("x", "y"))


def begin(points, rank, width, *args):
    tall, row = pltpu.VMEM((points, rank), F32), pltpu.VMEM((1, points), F32)
    packed = pltpu.VMEM((rank, 2 * width + LANES), F32)
    wide, block = in_vmem(points, width), in_vmem(rank + 8, points)
    half = in_vmem(rank // 2, 2 * width + LANES)
    return pl.pallas_call(
        begin_kernel,
        out_shape=[wide, wide, block, block, half, half],
        in_specs=[pl.BlockSpec(memory_space=pltpu.HBM)] * 6,
        scratch_shapes=[packed, tall, tall, row, row, pltpu.SemaphoreType.DMA((6,))],
        compiler_params=pltpu.CompilerParams(vmem_limit_bytes=VMEM),
    )(*[pltpu.with_memory_space_constraint(a, pltpu.HBM) for a in args])


def local(embed_source, embed_target, mass_source, mass_target, start_source, start_target):
    points, rank = start_source.shape
    width = embed_source.shape[1]
    line, sums_of, mid_of = in_vmem(8, rank), in_vmem(2, rank), in_vmem(1, rank)
    sums_in = in_vmem(lax.axis_size(("x", "core")), 2, rank)
    block, one, four = in_vmem(rank + 8, points), in_vmem(1, rank, points), in_vmem(4, rank, points)
    x, y, w1, w2, keep, send = begin(
        points,
        rank,
        width,
        embed_source,
        embed_target,
        start_source,
        start_target,
        mass_source[None],
        mass_target[None],
    )
    packed_shape = (rank, 2 * width + LANES)
    g1, g2, peak, small = call(
        lambda *refs: gradients_kernel(True, 1, *refs),
        [one, one, in_vmem(lax.axis_size(AXES), 1, LANES), line],
        *sum_columns(keep, send),
        x,
        y,
        w1,
        w2,
        scratch=[packed_shape],
    )
    k1, k2, kmid, sums = call(
        lambda *refs: first_step_kernel(True, 1, *refs),
        [block, block, mid_of, sums_in],
        g1,
        g2,
        swap(peak, AXES),
        small,
        w1,
        w2,
    )
    margins, (k1_1, k2_3) = sum_all(sums, [(k1, 1), (k2, 3)])
    sums, scale = call(lambda *refs: step_kernel(True, 1, *refs), [sums_in, sums_of], margins, kmid, k1, k2)
    margins, (k1_2, k2_2) = sum_all(sums, [(k1_1, 3), (k2_3, 1)])
    sums, scale = call(lambda *refs: step_kernel(False, 1, *refs), [sums_in, sums_of], margins, kmid, scale, k1, k2)
    margins, (k1_3, k2_1) = sum_all(sums, [(k1, 3), (k2, 1)])
    blocks = (k1, k1_1, k1_3, k1_2, k2, k2_1, k2_3, k2_2)
    step = lambda *refs: step_kernel(False, 4, *refs)
    for inner in range(3, INNER - 1):
        sums, scale = call(step, [sums_of, sums_of], margins, kmid, scale, *blocks)
        if inner == 3:
            margins, (x_1, y_3) = sum_rest(sums, [(x, 1), (y, 3)])
        elif inner == 4:
            margins, (x_2, y_2) = sum_rest(sums, [(x_1, 3), (y_3, 1)])
        elif inner == 5:
            margins, (x_3, y_1) = sum_rest(sums, [(x, 3), (y, 1)])
        else:
            margins, _ = sum_rest(sums)
    near = (x, x_1, x_3, x_2, y, y_1, y_3, y_2)
    rest = ("core", "z", "y")
    for outer in range(1, OUTER):
        quarter = in_vmem(rank // lax.axis_size("x"), 2 * width + LANES)
        factor, scale, packed = call(
            last_step_kernel, [in_vmem(8, points), sums_of, quarter], margins, kmid, scale, *near, *blocks
        )
        count = lax.axis_size(("core", "y"))
        packed = packed.reshape(count, packed.shape[0] // count, packed.shape[1])
        g1, g2, peak, small = call(
            lambda *refs: gradients_kernel(False, 4, *refs),
            [four, four, in_vmem(lax.axis_size(rest), 1, LANES), line],
            *sum_along(packed, ("core", "y")),
            scale,
            kmid,
            *near,
            *blocks,
            scratch=[packed_shape],
        )
        *blocks, kmid, sums = call(
            lambda *refs: first_step_kernel(False, 4, *refs),
            [block] * 8 + [mid_of, sums_of],
            g1,
            g2,
            swap(peak, rest),
            small,
            factor,
            *blocks,
        )
        margins, _ = sum_rest(sums)
        for inner in range(1, INNER - 1):
            before = () if inner == 1 else (scale,)
            sums, scale = call(
                lambda *refs: step_kernel(not before, 4, *refs), [sums_of, sums_of], margins, kmid, *before, *blocks
            )
            margins, _ = sum_rest(sums)
    sums, scale, factor = call(step, [sums_of, sums_of, in_vmem(2, points)], margins, kmid, scale, *blocks)
    margins, _ = sum_rest(sums)
    total = float(points * lax.axis_size(AXES) * rank)
    result = jax.ShapeDtypeStruct((points, rank), F32)
    left, right, middle = call(
        lambda *refs: end_kernel(total, *refs),
        [result, result, jax.ShapeDtypeStruct((1, rank), F32)],
        margins,
        kmid,
        scale,
        blocks[0],
        blocks[4],
        factor,
    )
    return left, right, middle[0]


def solution(mesh):
    mesh = Mesh(mesh.devices.reshape(4, 2, 8, 4), AXES)
    return jax.shard_map(
        local,
        mesh=mesh,
        in_specs=(P(AXES, None), P(AXES, None), P(AXES), P(AXES), P(AXES, None), P(AXES, None)),
        out_specs=(P(AXES, None), P(AXES, None), P()),
        check_vma=False,
    )
```

```python
import jax
import jax.numpy as jnp
from jax import lax
from jax.experimental import pallas as pl
from jax.experimental.pallas import tpu as pltpu
from jax.sharding import Mesh, PartitionSpec as P

OUTER = 2
INNER = 8
LANES = 128
VMEM = 8 * 2**20
AXES = ("x", "core", "z", "y")
HIGH = lax.Precision.HIGHEST
F32 = jnp.float32


def chunks(n):
    return [slice(j, j + LANES) for j in range(0, n, LANES)]


def column(row):
    return jnp.transpose(jnp.broadcast_to(row, (LANES, row.shape[1])))


def row_of(partial):
    return jnp.sum(jnp.transpose(partial), 0, keepdims=True)


def widen(col, n):
    return jnp.concatenate([col] * (n // LANES), 1)


def pack(weights, embeds, norms, packed_ref, extra):
    rank, width = packed_ref.shape[0], embeds[0][0].shape[1]
    lane = lax.broadcasted_iota(jnp.int32, (rank, LANES), 1)
    small = jnp.zeros((rank, LANES), F32)
    for s in range(2):
        product = heavy = plain = 0.0
        for w, e, n in zip(weights, embeds, norms):
            product = product + jnp.dot(w[s], e[s], precision=HIGH, preferred_element_type=F32)
            heavy = heavy + jnp.sum(w[s] * n[s], 1, keepdims=True)
            plain = plain + jnp.sum(w[s], 1, keepdims=True)
        packed_ref[:, s * width : (s + 1) * width] = product
        small = jnp.where(lane == 2 * s, heavy, small)
        small = jnp.where(lane == 2 * s + 1, plain, small)
    for n, value in enumerate(extra):
        small = jnp.where(lane == 4 + n, value, small)
    packed_ref[:, 2 * width :] = small


def norms_of(embed):
    ones = jnp.ones((8, embed.shape[1]), F32)
    square = embed * embed
    return lax.dot_general(ones, square, (((1,), (1,)), ((), ())), precision=HIGH, preferred_element_type=F32)[:1]


def halves(ref):
    half = ref.shape[0] // 2
    core = lax.axis_index("core")
    return [pl.ds(pl.multiple_of(c * half, 8), half) for c in (core, 1 - core)]


def begin_kernel(
    x_in,
    y_in,
    a_in,
    b_in,
    m1_in,
    m2_in,
    x_ref,
    y_ref,
    w1_ref,
    w2_ref,
    keep_ref,
    send_ref,
    packed_ref,
    a_ref,
    b_ref,
    m1_ref,
    m2_ref,
    sems,
):
    pairs = ((m1_in, m1_ref), (m2_in, m2_ref), (a_in, a_ref), (x_in, x_ref), (b_in, b_ref), (y_in, y_ref))
    copies = [pltpu.make_async_copy(source, target, sems.at[n]) for n, (source, target) in enumerate(pairs)]
    for copy in copies:
        copy.start()
    for copy in copies:
        copy.wait()
    embeds, weights, norms, totals = [], [], [], []
    for e_ref, f_ref, m_ref, w_ref in ((x_ref, a_ref, m1_ref, w1_ref), (y_ref, b_ref, m2_ref, w2_ref)):
        factor = jnp.transpose(f_ref[...])
        rank = factor.shape[0]
        mass = m_ref[...]
        weight = factor * (mass / jnp.sum(factor, 0, keepdims=True))
        embeds.append(e_ref[...])
        weights.append(weight)
        norms.append(norms_of(embeds[-1]))
        totals.append(jnp.sum(mass, 1, keepdims=True))
        w_ref[:rank, :] = weight
        w_ref[rank : rank + 1, :] = mass
        w_ref[rank + 1 :, :] = jnp.broadcast_to(norms[-1], (w_ref.shape[0] - rank - 1, mass.shape[1]))
    pack([weights], [embeds], [norms], packed_ref, totals)
    mine, others = halves(packed_ref)
    keep_ref[...] = packed_ref[mine, :]
    send_ref[...] = packed_ref[others, :]


def fold_kernel(in_ref, out_ref):
    out_ref[...] = jnp.broadcast_to(jnp.sum(in_ref[...], 0, keepdims=True), out_ref.shape)


def add_kernel(a_ref, b_ref, out_ref):
    value = a_ref[...] + b_ref[...]
    out_ref[...] = value if value.shape == out_ref.shape else jnp.broadcast_to(value[None], out_ref.shape)


def summed(full_ref, inverse, middle):
    rank = full_ref.shape[0]
    width = (full_ref.shape[1] - LANES) // 2
    small = full_ref[:, 2 * width :]
    cross = [full_ref[:, s * width : (s + 1) * width] * widen(inverse[s], width) for s in range(2)]
    heavy = [small[:, 2 * s : 2 * s + 1] * inverse[s] for s in range(2)]
    plain = [small[:, 2 * s + 1 : 2 * s + 2] * inverse[s] for s in range(2)]
    diagonal = heavy[0] * plain[1] + plain[0] * heavy[1] - 2.0 * jnp.sum(cross[0] * cross[1], 1, keepdims=True)
    return cross, heavy, plain, 1.0 / middle, -diagonal / (middle * middle)


def gradient(terms, s, embed, norm, grad_ref, peak):
    cross, heavy, plain, over, _ = terms
    width = embed.shape[1]
    product = lax.dot_general(
        cross[1 - s] * widen(-2.0 * over, width),
        embed,
        (((1,), (1,)), ((), ())),
        precision=HIGH,
        preferred_element_type=F32,
    )
    points = product.shape[1]
    grad = product + widen(plain[1 - s] * over, points) * norm + widen(heavy[1 - s] * over, points)
    grad_ref[...] = grad
    for c in chunks(points):
        peak = jnp.maximum(peak, jnp.max(jnp.abs(grad[:, c]), 0, keepdims=True))
    return peak


def rows(columns):
    n = columns[0].shape[0]
    lane = lax.broadcasted_iota(jnp.int32, (n, LANES), 1)
    block = jnp.zeros((n, LANES), F32)
    for i, c in enumerate(columns):
        block = jnp.where(lane == i, c, block)
    return jnp.transpose(block)[:8]


def gradients_kernel(first, n, own_ref, other_ref, *refs):
    before, refs = ((), refs) if first else (refs[:2], refs[2:])
    e_refs, k_refs = refs[: 2 * n], refs[2 * n : 4 * n]
    g1_ref, g2_ref, peak_ref, rows_ref, full_ref = refs[4 * n :]
    rank, width = full_ref.shape[0], e_refs[0].shape[1]
    mine, others = halves(full_ref)
    full_ref[mine, :] = own_ref[...]
    full_ref[others, :] = other_ref[...]

    def small(i):
        return jnp.broadcast_to(full_ref[:, 2 * width + i : 2 * width + i + 1], (rank, LANES))

    if first:
        inverse = [1.0 / small(4), 1.0 / small(5)]
        middle = jnp.full((rank, LANES), 1.0 / rank, F32)
    else:
        scale_ref, kmid_ref = before
        marg = [small(1), small(3)]
        scale = [column(scale_ref[s : s + 1, :]) for s in range(2)]
        middle = cube_root(column(kmid_ref[...]) * scale[0] * marg[0] * scale[1] * marg[1])
        inverse = [middle / marg[s] for s in range(2)]
    terms = summed(full_ref, inverse, middle)
    peak = jnp.max(jnp.abs(terms[-1]), 0, keepdims=True)
    for s, g_ref in enumerate((g1_ref, g2_ref)):
        for j in range(n):
            norm = k_refs[n * s + j][rank + 1 : rank + 2, :]
            peak = gradient(terms, s, e_refs[n * s + j][...], norm, g_ref.at[j], peak)
    peak_ref[...] = jnp.broadcast_to(peak[None], peak_ref.shape)
    rows_ref[...] = rows([middle, terms[-1], inverse[0], inverse[1]])


def cube_root(value):
    return jnp.exp(jnp.log(value) * (1.0 / 3.0))


def rescale(margins_ref, kmid_ref, scale_ref):
    margins = jnp.sum(margins_ref[...], 0)
    first, second = margins[0:1], margins[1:2]
    if scale_ref is None:
        middle = cube_root(kmid_ref[...] * first * second)
    else:
        middle = cube_root(kmid_ref[...] * scale_ref[0:1, :] * first * scale_ref[1:2, :] * second)
    return middle, [middle / first, middle / second]


def scaling(k_refs, rank, scale):
    groups = [slice(i, i + 8) for i in range(0, rank, 8)]
    points = k_refs[0].shape[1]
    totals = [jnp.zeros((8, points), F32) for _ in k_refs]
    for i in groups:
        wide = None if scale is None else widen(scale[i], points)
        for j, k_ref in enumerate(k_refs):
            totals[j] = totals[j] + (k_ref[i, :] if scale is None else k_ref[i, :] * wide)
    factors = [
        k_ref[rank : rank + 1, :] / jnp.sum(total, 0, keepdims=True) for k_ref, total in zip(k_refs, totals)
    ]
    wides = [jnp.broadcast_to(factor, (8, points)) for factor in factors]
    partials = []
    for i in groups:
        parts = []
        for k_ref, wide in zip(k_refs, wides):
            product = k_ref[i, :] * wide
            part = product[:, :LANES]
            for c in chunks(points)[1:]:
                part = part + product[:, c]
            parts.append(part)
        pairs = [sum(parts[j + 1 : j + 2], parts[j]) for j in range(0, len(parts), 2)]
        partials.append(sum(pairs[1:], pairs[0]))
    return factors, row_of(jnp.concatenate(partials, 0))


def rate_of(peak_ref):
    peak = jnp.max(jnp.max(peak_ref[...], 0), 1, keepdims=True)
    return 30.0 / (peak * peak + 1e-06)


def first_step_kernel(first, n, g1_ref, g2_ref, peak_ref, rows_ref, *refs):
    factors, refs = ((), refs) if first else (refs[:1], refs[1:])
    old_refs, new_refs, (kmid_ref, sums_ref) = refs[: 2 * n], refs[2 * n : 4 * n], refs[4 * n :]
    rank = g1_ref.shape[1]
    rate = rate_of(peak_ref)
    kmid_ref[...] = rows_ref[0:1, :] * jnp.exp(-rate * rows_ref[1:2, :])
    for s, g_ref in enumerate((g1_ref, g2_ref)):
        inverse = column(rows_ref[2 + s : 3 + s, :])
        for j in range(n):
            b = n * s + j
            old_ref, new_ref = old_refs[b], new_refs[b]
            for c in chunks(old_ref.shape[1]):
                old = old_ref[:rank, c]
                for ref in factors:
                    old = old * ref[b : b + 1, c]
                new_ref[:rank, c] = (old * inverse) * jnp.exp(-rate * g_ref[j, :, c])
            new_ref[rank:, :] = old_ref[rank:, :]
            if first:
                new_ref[rank : rank + 1, :] = old_ref[rank : rank + 1, :] * rows_ref[2 + s : 3 + s, 0:1]
        _, row = scaling(new_refs[n * s : n * s + n], rank, None)
        put(sums_ref, s, row)


def step_kernel(initial, n, margins_ref, kmid_ref, *refs):
    scale_ref, refs = (None, refs) if initial else (refs[0], refs[1:])
    k_refs, sums_ref, new_ref, factor_refs = refs[: 2 * n], refs[2 * n], refs[2 * n + 1], refs[2 * n + 2 :]
    rank = kmid_ref.shape[1]
    _, scales = rescale(margins_ref, kmid_ref, scale_ref)
    for s in range(2):
        new_ref[s : s + 1, :] = scales[s]
        factors, row = scaling(k_refs[n * s : n * s + n], rank, column(scales[s]))
        put(sums_ref, s, row)
        for ref in factor_refs:
            ref[s : s + 1, :] = factors[0]


def put(sums_ref, s, row):
    if len(sums_ref.shape) == 2:
        sums_ref[s : s + 1, :] = row
    else:
        sums_ref[:, s : s + 1, :] = jnp.broadcast_to(row[None], (sums_ref.shape[0],) + row.shape)


def last_step_kernel(margins_ref, kmid_ref, scale_ref, *refs):
    e_refs, k_refs, (factor_ref, new_ref, packed_ref) = refs[:8], refs[8:16], refs[16:]
    rank, part = kmid_ref.shape[1], packed_ref.shape[0] // 2
    ours = [pl.ds(pl.multiple_of(c * (rank // 2) + lax.axis_index("x") * part, 8), part) for c in range(2)]
    weights = [[None, None] for _ in range(4)]
    norms = [[None, None] for _ in range(4)]
    _, scales = rescale(margins_ref, kmid_ref, scale_ref)
    for s in range(2):
        new_ref[s : s + 1, :] = scales[s]
        scale = column(scales[s])
        for j in range(4):
            n = 4 * s + j
            k_ref = k_refs[n]
            for c in chunks(k_ref.shape[1]):
                total = jnp.sum(k_ref[:rank, c] * scale, 0, keepdims=True)
                factor_ref[n : n + 1, c] = k_ref[rank : rank + 1, c] / total
            weights[j][s] = jnp.concatenate([k_ref[o, :] for o in ours], 0) * factor_ref[n : n + 1, :]
            norms[j][s] = k_ref[rank + 1 : rank + 2, :]
    embeds = [(e_refs[j][...], e_refs[4 + j][...]) for j in range(4)]
    pack(weights, embeds, norms, packed_ref, [])


def end_kernel(total, margins_ref, kmid_ref, scale_ref, k1_ref, k2_ref, factor_ref, o1_ref, o2_ref, middle_ref):
    rank = kmid_ref.shape[1]
    middle, scales = rescale(margins_ref, kmid_ref, scale_ref)
    middle_ref[...] = middle * float(rank)
    for s, (k_ref, o_ref) in enumerate(((k1_ref, o1_ref), (k2_ref, o2_ref))):
        scale = column(scales[s])
        for c in chunks(k_ref.shape[1]):
            value = (k_ref[:rank, c] * factor_ref[s : s + 1, c]) * scale * total
            o_ref[c, :] = jnp.transpose(value)


def split_kernel(a_ref, b_ref, first_ref, second_ref):
    value = a_ref[...] + b_ref[...]
    first_ref[...], second_ref[...] = value[0:1], value[1:2]


def join_kernel(a_ref, b_ref, c_ref, d_ref, out_ref):
    for s, value in enumerate((a_ref[...] + b_ref[...], c_ref[...] + d_ref[...])):
        put(out_ref, s, value)


def in_vmem(*shape):
    return pltpu.VMEM(shape, F32)


def to_vmem(array):
    return pltpu.with_memory_space_constraint(array, pltpu.VMEM)


def call(kernel, outs, *args, scratch=()):
    return pl.pallas_call(
        kernel,
        out_shape=outs,
        scratch_shapes=[pltpu.VMEM(shape, F32) for shape in scratch],
        compiler_params=pltpu.CompilerParams(vmem_limit_bytes=VMEM),
    )(*[to_vmem(a) for a in args])


def across(value, bits):
    return lax.ppermute(value, "x", [(i, i ^ bits) for i in range(lax.axis_size("x"))])


def swap(value, axes):
    return lax.all_to_all(value, axes, 0, 0)


def beside(value, axes, sends):
    if not sends:
        return swap(value, axes), []
    blocks, value = lax.optimization_barrier(([block for block, _ in sends], value))
    got = [across(block, bits) for block, (_, bits) in zip(blocks, sends)]
    return lax.optimization_barrier((swap(value, axes), got))


def sum_all(value, sends):
    value = swap(value, ("x", "core"))
    (value,) = call(fold_kernel, [in_vmem(lax.axis_size(("z", "y")), *value.shape[1:])], value)
    return beside(value, ("z", "y"), sends)


def other_core(value):
    return lax.ppermute(value, "core", [(0, 1), (1, 0)])


def sum_pairs(value, sends):
    row = in_vmem(1, value.shape[1])
    first, second = call(split_kernel, [row, row], value, other_core(value))
    pairs = (first, across(first, 3), second, across(second, 1))
    (value,) = call(join_kernel, [in_vmem(lax.axis_size(("z", "y")), *value.shape)], *pairs)
    return beside(value, ("z", "y"), sends)


def sum_rest(value, sends=()):
    (value,) = call(add_kernel, [in_vmem(lax.axis_size(("z", "y")), *value.shape)], value, other_core(value))
    return beside(value, ("z", "y"), sends)


def sum_along(part, axes):
    deep, wide, shape = lax.axis_size("z"), lax.axis_size(("x", "y")), part.shape[1:]
    (part,) = call(fold_kernel, [in_vmem(deep, *shape)], swap(part, axes))
    (part,) = call(fold_kernel, [in_vmem(wide, *shape)], swap(part, "z"))
    own = swap(part, ("x", "y")).reshape(wide * shape[0], shape[1])
    return own, other_core(own)


def sum_columns(keep, send):
    (part,) = call(add_kernel, [in_vmem(*keep.shape)], keep, other_core(send))
    count = lax.axis_size(("x", "y"))
    return sum_along(part.reshape(count, keep.shape[0] // count, keep.shape[1]), ("x", "y"))


def begin(points, rank, width, *args):
    tall, row = pltpu.VMEM((points, rank), F32), pltpu.VMEM((1, points), F32)
    packed = pltpu.VMEM((rank, 2 * width + LANES), F32)
    wide, block = in_vmem(points, width), in_vmem(rank + 8, points)
    half = in_vmem(rank // 2, 2 * width + LANES)
    return pl.pallas_call(
        begin_kernel,
        out_shape=[wide, wide, block, block, half, half],
        in_specs=[pl.BlockSpec(memory_space=pltpu.HBM)] * 6,
        scratch_shapes=[packed, tall, tall, row, row, pltpu.SemaphoreType.DMA((6,))],
        compiler_params=pltpu.CompilerParams(vmem_limit_bytes=VMEM),
    )(*[pltpu.with_memory_space_constraint(a, pltpu.HBM) for a in args])


def local(embed_source, embed_target, mass_source, mass_target, start_source, start_target):
    points, rank = start_source.shape
    width = embed_source.shape[1]
    line, sums_of, mid_of = in_vmem(8, rank), in_vmem(2, rank), in_vmem(1, rank)
    sums_in = in_vmem(lax.axis_size(("x", "core")), 2, rank)
    block, one, four = in_vmem(rank + 8, points), in_vmem(1, rank, points), in_vmem(4, rank, points)
    x, y, w1, w2, keep, send = begin(
        points,
        rank,
        width,
        embed_source,
        embed_target,
        start_source,
        start_target,
        mass_source[None],
        mass_target[None],
    )
    packed_shape = (rank, 2 * width + LANES)
    g1, g2, peak, small = call(
        lambda *refs: gradients_kernel(True, 1, *refs),
        [one, one, in_vmem(lax.axis_size(AXES), 1, LANES), line],
        *sum_columns(keep, send),
        x,
        y,
        w1,
        w2,
        scratch=[packed_shape],
    )
    k1, k2, kmid, sums = call(
        lambda *refs: first_step_kernel(True, 1, *refs),
        [block, block, mid_of, sums_in],
        g1,
        g2,
        swap(peak, AXES),
        small,
        w1,
        w2,
    )
    margins, (k1_1, k2_3) = sum_all(sums, [(k1, 1), (k2, 3)])
    pairs = (k1, k1_1, k2, k2_3)
    sums, scale = call(lambda *refs: step_kernel(True, 2, *refs), [sums_of, sums_of], margins, kmid, *pairs)
    margins, (k1_2, k2_2) = sum_pairs(sums, [(k1_1, 3), (k2_3, 1)])
    sums, scale = call(lambda *refs: step_kernel(False, 2, *refs), [sums_of, sums_of], margins, kmid, scale, *pairs)
    margins, (k1_3, k2_1) = sum_pairs(sums, [(k1, 3), (k2, 1)])
    blocks = (k1, k1_1, k1_3, k1_2, k2, k2_1, k2_3, k2_2)
    step = lambda *refs: step_kernel(False, 4, *refs)
    for inner in range(3, INNER - 1):
        sums, scale = call(step, [sums_of, sums_of], margins, kmid, scale, *blocks)
        if inner == 3:
            margins, (x_1, y_3) = sum_rest(sums, [(x, 1), (y, 3)])
        elif inner == 4:
            margins, (x_2, y_2) = sum_rest(sums, [(x_1, 3), (y_3, 1)])
        elif inner == 5:
            margins, (x_3, y_1) = sum_rest(sums, [(x, 3), (y, 1)])
        else:
            margins, _ = sum_rest(sums)
    near = (x, x_1, x_3, x_2, y, y_1, y_3, y_2)
    rest = ("core", "z", "y")
    for outer in range(1, OUTER):
        quarter = in_vmem(rank // lax.axis_size("x"), 2 * width + LANES)
        factor, scale, packed = call(
            last_step_kernel, [in_vmem(8, points), sums_of, quarter], margins, kmid, scale, *near, *blocks
        )
        count = lax.axis_size(("core", "y"))
        packed = packed.reshape(count, packed.shape[0] // count, packed.shape[1])
        g1, g2, peak, small = call(
            lambda *refs: gradients_kernel(False, 4, *refs),
            [four, four, in_vmem(lax.axis_size(rest), 1, LANES), line],
            *sum_along(packed, ("core", "y")),
            scale,
            kmid,
            *near,
            *blocks,
            scratch=[packed_shape],
        )
        *blocks, kmid, sums = call(
            lambda *refs: first_step_kernel(False, 4, *refs),
            [block] * 8 + [mid_of, sums_of],
            g1,
            g2,
            swap(peak, rest),
            small,
            factor,
            *blocks,
        )
        margins, _ = sum_rest(sums)
        for inner in range(1, INNER - 1):
            before = () if inner == 1 else (scale,)
            sums, scale = call(
                lambda *refs: step_kernel(not before, 4, *refs), [sums_of, sums_of], margins, kmid, *before, *blocks
            )
            margins, _ = sum_rest(sums)
    sums, scale, factor = call(step, [sums_of, sums_of, in_vmem(2, points)], margins, kmid, scale, *blocks)
    margins, _ = sum_rest(sums)
    total = float(points * lax.axis_size(AXES) * rank)
    result = jax.ShapeDtypeStruct((points, rank), F32)
    left, right, middle = call(
        lambda *refs: end_kernel(total, *refs),
        [result, result, jax.ShapeDtypeStruct((1, rank), F32)],
        margins,
        kmid,
        scale,
        blocks[0],
        blocks[4],
        factor,
    )
    return left, right, middle[0]


def solution(mesh):
    mesh = Mesh(mesh.devices.reshape(4, 2, 8, 4), AXES)
    return jax.shard_map(
        local,
        mesh=mesh,
        in_specs=(P(AXES, None), P(AXES, None), P(AXES), P(AXES), P(AXES, None), P(AXES, None)),
        out_specs=(P(AXES, None), P(AXES, None), P()),
        check_vma=False,
    )
```

```python
import jax
import jax.numpy as jnp
from jax import lax
from jax.experimental import pallas as pl
from jax.experimental.pallas import tpu as pltpu
from jax.sharding import Mesh, PartitionSpec as P

OUTER = 2
INNER = 8
LANES = 128
VMEM = 8 * 2**20
AXES = ("x", "core", "z", "y")
HIGH = lax.Precision.HIGHEST
F32 = jnp.float32


def chunks(n):
    return [slice(j, j + LANES) for j in range(0, n, LANES)]


def column(row):
    return jnp.transpose(jnp.broadcast_to(row, (LANES, row.shape[1])))


def row_of(partial):
    return jnp.sum(jnp.transpose(partial), 0, keepdims=True)


def widen(col, n):
    return jnp.concatenate([col] * (n // LANES), 1)


def pack(weights, embeds, norms, packed_ref, extra):
    rank, width = packed_ref.shape[0], embeds[0][0].shape[1]
    lane = lax.broadcasted_iota(jnp.int32, (rank, LANES), 1)
    small = jnp.zeros((rank, LANES), F32)
    for s in range(2):
        product = heavy = plain = 0.0
        for w, e, n in zip(weights, embeds, norms):
            product = product + jnp.dot(w[s], e[s], precision=HIGH, preferred_element_type=F32)
            heavy = heavy + jnp.sum(w[s] * n[s], 1, keepdims=True)
            plain = plain + jnp.sum(w[s], 1, keepdims=True)
        packed_ref[:, s * width : (s + 1) * width] = product
        small = jnp.where(lane == 2 * s, heavy, small)
        small = jnp.where(lane == 2 * s + 1, plain, small)
    for n, value in enumerate(extra):
        small = jnp.where(lane == 4 + n, value, small)
    packed_ref[:, 2 * width :] = small


def norms_of(embed):
    ones = jnp.ones((8, embed.shape[1]), F32)
    square = embed * embed
    return lax.dot_general(ones, square, (((1,), (1,)), ((), ())), precision=HIGH, preferred_element_type=F32)[:1]


def halves(ref):
    half = ref.shape[0] // 2
    core = lax.axis_index("core")
    return [pl.ds(pl.multiple_of(c * half, 8), half) for c in (core, 1 - core)]


def begin_kernel(
    x_in,
    y_in,
    a_in,
    b_in,
    m1_in,
    m2_in,
    x_ref,
    y_ref,
    w1_ref,
    w2_ref,
    keep_ref,
    send_ref,
    packed_ref,
    a_ref,
    b_ref,
    m1_ref,
    m2_ref,
    sems,
):
    pairs = ((m1_in, m1_ref), (m2_in, m2_ref), (a_in, a_ref), (x_in, x_ref), (b_in, b_ref), (y_in, y_ref))
    copies = [pltpu.make_async_copy(source, target, sems.at[n]) for n, (source, target) in enumerate(pairs)]
    for copy in copies:
        copy.start()
    for copy in copies:
        copy.wait()
    embeds, weights, norms, totals = [], [], [], []
    for e_ref, f_ref, m_ref, w_ref in ((x_ref, a_ref, m1_ref, w1_ref), (y_ref, b_ref, m2_ref, w2_ref)):
        factor = jnp.transpose(f_ref[...])
        rank = factor.shape[0]
        mass = m_ref[...]
        weight = factor * (mass / jnp.sum(factor, 0, keepdims=True))
        embeds.append(e_ref[...])
        weights.append(weight)
        norms.append(norms_of(embeds[-1]))
        totals.append(jnp.sum(mass, 1, keepdims=True))
        w_ref[:rank, :] = weight
        w_ref[rank : rank + 1, :] = mass
        w_ref[rank + 1 :, :] = jnp.broadcast_to(norms[-1], (w_ref.shape[0] - rank - 1, mass.shape[1]))
    pack([weights], [embeds], [norms], packed_ref, totals)
    mine, others = halves(packed_ref)
    keep_ref[...] = packed_ref[mine, :]
    send_ref[...] = packed_ref[others, :]


def fold_kernel(in_ref, out_ref):
    out_ref[...] = jnp.broadcast_to(jnp.sum(in_ref[...], 0, keepdims=True), out_ref.shape)


def add_kernel(a_ref, b_ref, out_ref):
    value = a_ref[...] + b_ref[...]
    out_ref[...] = value if value.shape == out_ref.shape else jnp.broadcast_to(value[None], out_ref.shape)


def summed(full_ref, inverse, middle):
    rank = full_ref.shape[0]
    width = (full_ref.shape[1] - LANES) // 2
    small = full_ref[:, 2 * width :]
    cross = [full_ref[:, s * width : (s + 1) * width] * widen(inverse[s], width) for s in range(2)]
    heavy = [small[:, 2 * s : 2 * s + 1] * inverse[s] for s in range(2)]
    plain = [small[:, 2 * s + 1 : 2 * s + 2] * inverse[s] for s in range(2)]
    diagonal = heavy[0] * plain[1] + plain[0] * heavy[1] - 2.0 * jnp.sum(cross[0] * cross[1], 1, keepdims=True)
    return cross, heavy, plain, 1.0 / middle, -diagonal / (middle * middle)


def gradient(terms, s, embed, norm, grad_ref, peak):
    cross, heavy, plain, over, _ = terms
    width = embed.shape[1]
    product = lax.dot_general(
        cross[1 - s] * widen(-2.0 * over, width),
        embed,
        (((1,), (1,)), ((), ())),
        precision=HIGH,
        preferred_element_type=F32,
    )
    points = product.shape[1]
    grad = product + widen(plain[1 - s] * over, points) * norm + widen(heavy[1 - s] * over, points)
    grad_ref[...] = grad
    for c in chunks(points):
        peak = jnp.maximum(peak, jnp.max(jnp.abs(grad[:, c]), 0, keepdims=True))
    return peak


def rows(columns):
    n = columns[0].shape[0]
    lane = lax.broadcasted_iota(jnp.int32, (n, LANES), 1)
    block = jnp.zeros((n, LANES), F32)
    for i, c in enumerate(columns):
        block = jnp.where(lane == i, c, block)
    return jnp.transpose(block)[:8]


def half_of(which, rank):
    core = lax.axis_index("core")
    return pl.ds(pl.multiple_of((core if which == 0 else 1 - core) * (rank // 2), LANES), rank // 2)


def gradients_kernel(first, n, which, sum_ref, *refs):
    before, refs = ((), refs) if first else (refs[:2], refs[2:])
    prior, refs = ((), refs) if which == 0 else (refs[:1], refs[1:])
    e_refs, k_refs = refs[: 2 * n], refs[2 * n : 4 * n]
    g1_ref, g2_ref, peak_ref, rows_ref = refs[4 * n :]
    half, width = sum_ref.shape[0], e_refs[0].shape[1]
    rank = 2 * half

    def small(i):
        return jnp.broadcast_to(sum_ref[:, 2 * width + i : 2 * width + i + 1], (half, LANES))

    if first:
        inverse = [1.0 / small(4), 1.0 / small(5)]
        middle = jnp.full((half, LANES), 1.0 / rank, F32)
    else:
        scale_ref, kmid_ref = before
        ours = half_of(which, rank)
        marg = [small(1), small(3)]
        scale = [column(scale_ref[s : s + 1, ours]) for s in range(2)]
        middle = cube_root(column(kmid_ref[0:1, ours]) * scale[0] * marg[0] * scale[1] * marg[1])
        inverse = [middle / marg[s] for s in range(2)]
    terms = summed(sum_ref, inverse, middle)
    peak = jnp.max(jnp.abs(terms[-1]), 0, keepdims=True)
    for ref in prior:
        peak = jnp.maximum(peak, ref[...])
    for s, g_ref in enumerate((g1_ref, g2_ref)):
        for j in range(n):
            norm = k_refs[n * s + j][rank + 1 : rank + 2, :]
            peak = gradient(terms, s, e_refs[n * s + j][...], norm, g_ref.at[j], peak)
    peak_ref[...] = peak if which == 0 else jnp.broadcast_to(peak[None], peak_ref.shape)
    rows_ref[...] = rows([middle, terms[-1], inverse[0], inverse[1]])


def cube_root(value):
    return jnp.exp(jnp.log(value) * (1.0 / 3.0))


def rescale(margins_ref, kmid_ref, scale_ref):
    margins = jnp.sum(margins_ref[...], 0)
    first, second = margins[0:1], margins[1:2]
    if scale_ref is None:
        middle = cube_root(kmid_ref[...] * first * second)
    else:
        middle = cube_root(kmid_ref[...] * scale_ref[0:1, :] * first * scale_ref[1:2, :] * second)
    return middle, [middle / first, middle / second]


def scaling(k_refs, rank, scale):
    groups = [slice(i, i + 8) for i in range(0, rank, 8)]
    points = k_refs[0].shape[1]
    totals = [jnp.zeros((8, points), F32) for _ in k_refs]
    for i in groups:
        wide = None if scale is None else widen(scale[i], points)
        for j, k_ref in enumerate(k_refs):
            totals[j] = totals[j] + (k_ref[i, :] if scale is None else k_ref[i, :] * wide)
    factors = [
        k_ref[rank : rank + 1, :] / jnp.sum(total, 0, keepdims=True) for k_ref, total in zip(k_refs, totals)
    ]
    wides = [jnp.broadcast_to(factor, (8, points)) for factor in factors]
    partials = []
    for i in groups:
        parts = []
        for k_ref, wide in zip(k_refs, wides):
            product = k_ref[i, :] * wide
            part = product[:, :LANES]
            for c in chunks(points)[1:]:
                part = part + product[:, c]
            parts.append(part)
        pairs = [sum(parts[j + 1 : j + 2], parts[j]) for j in range(0, len(parts), 2)]
        partials.append(sum(pairs[1:], pairs[0]))
    return factors, row_of(jnp.concatenate(partials, 0))


def rate_of(peak_ref):
    peak = jnp.max(jnp.max(peak_ref[...], 0), 1, keepdims=True)
    return 30.0 / (peak * peak + 1e-06)


def first_step_kernel(first, n, peak_ref, *refs):
    parts, refs = (refs[:3], refs[3:6]), refs[6:]
    factors, refs = ((), refs) if first else (refs[:1], refs[1:])
    old_refs, new_refs, (kmid_ref, sums_ref) = refs[: 2 * n], refs[2 * n : 4 * n], refs[4 * n :]
    rank = kmid_ref.shape[1]
    rate = rate_of(peak_ref)
    for which, (g1_ref, g2_ref, rows_ref) in enumerate(parts):
        ours = half_of(which, rank)
        kmid_ref[0:1, ours] = rows_ref[0:1, :] * jnp.exp(-rate * rows_ref[1:2, :])
        for s, g_ref in enumerate((g1_ref, g2_ref)):
            inverse = column(rows_ref[2 + s : 3 + s, :])
            for j in range(n):
                b = n * s + j
                for c in chunks(old_refs[b].shape[1]):
                    old = old_refs[b][ours, c]
                    for ref in factors:
                        old = old * ref[b : b + 1, c]
                    new_refs[b][ours, c] = (old * inverse) * jnp.exp(-rate * g_ref[j, :, c])
    rows_ref = parts[0][2]
    for s in range(2):
        for b in range(n * s, n * s + n):
            new_refs[b][rank:, :] = old_refs[b][rank:, :]
            if first:
                new_refs[b][rank : rank + 1, :] = old_refs[b][rank : rank + 1, :] * rows_ref[2 + s : 3 + s, 0:1]
        _, row = scaling(new_refs[n * s : n * s + n], rank, None)
        put(sums_ref, s, row)


def step_kernel(initial, n, margins_ref, kmid_ref, *refs):
    scale_ref, refs = (None, refs) if initial else (refs[0], refs[1:])
    k_refs, sums_ref, new_ref, factor_refs = refs[: 2 * n], refs[2 * n], refs[2 * n + 1], refs[2 * n + 2 :]
    rank = kmid_ref.shape[1]
    _, scales = rescale(margins_ref, kmid_ref, scale_ref)
    for s in range(2):
        new_ref[s : s + 1, :] = scales[s]
        factors, row = scaling(k_refs[n * s : n * s + n], rank, column(scales[s]))
        put(sums_ref, s, row)
        for ref in factor_refs:
            ref[s : s + 1, :] = factors[0]


def put(sums_ref, s, row):
    if len(sums_ref.shape) == 2:
        sums_ref[s : s + 1, :] = row
    else:
        sums_ref[:, s : s + 1, :] = jnp.broadcast_to(row[None], (sums_ref.shape[0],) + row.shape)


def last_step_kernel(margins_ref, kmid_ref, scale_ref, *refs):
    e_refs, k_refs, (factor_ref, new_ref, packed_ref) = refs[:8], refs[8:16], refs[16:]
    rank, part = kmid_ref.shape[1], packed_ref.shape[0] // 2
    ours = [pl.ds(pl.multiple_of(c * (rank // 2) + lax.axis_index("x") * part, 8), part) for c in range(2)]
    weights = [[None, None] for _ in range(4)]
    norms = [[None, None] for _ in range(4)]
    _, scales = rescale(margins_ref, kmid_ref, scale_ref)
    for s in range(2):
        new_ref[s : s + 1, :] = scales[s]
        scale = column(scales[s])
        for j in range(4):
            n = 4 * s + j
            k_ref = k_refs[n]
            for c in chunks(k_ref.shape[1]):
                total = jnp.sum(k_ref[:rank, c] * scale, 0, keepdims=True)
                factor_ref[n : n + 1, c] = k_ref[rank : rank + 1, c] / total
            weights[j][s] = jnp.concatenate([k_ref[o, :] for o in ours], 0) * factor_ref[n : n + 1, :]
            norms[j][s] = k_ref[rank + 1 : rank + 2, :]
    embeds = [(e_refs[j][...], e_refs[4 + j][...]) for j in range(4)]
    pack(weights, embeds, norms, packed_ref, [])


def end_kernel(total, margins_ref, kmid_ref, scale_ref, k1_ref, k2_ref, factor_ref, o1_ref, o2_ref, middle_ref):
    rank = kmid_ref.shape[1]
    middle, scales = rescale(margins_ref, kmid_ref, scale_ref)
    middle_ref[...] = middle * float(rank)
    for s, (k_ref, o_ref) in enumerate(((k1_ref, o1_ref), (k2_ref, o2_ref))):
        scale = column(scales[s])
        for c in chunks(k_ref.shape[1]):
            value = (k_ref[:rank, c] * factor_ref[s : s + 1, c]) * scale * total
            o_ref[c, :] = jnp.transpose(value)


def split_kernel(a_ref, b_ref, first_ref, second_ref):
    value = a_ref[...] + b_ref[...]
    first_ref[...], second_ref[...] = value[0:1], value[1:2]


def join_kernel(a_ref, b_ref, c_ref, d_ref, out_ref):
    for s, value in enumerate((a_ref[...] + b_ref[...], c_ref[...] + d_ref[...])):
        put(out_ref, s, value)


def in_vmem(*shape):
    return pltpu.VMEM(shape, F32)


def to_vmem(array):
    return pltpu.with_memory_space_constraint(array, pltpu.VMEM)


def call(kernel, outs, *args, scratch=()):
    return pl.pallas_call(
        kernel,
        out_shape=outs,
        scratch_shapes=[pltpu.VMEM(shape, F32) for shape in scratch],
        compiler_params=pltpu.CompilerParams(vmem_limit_bytes=VMEM),
    )(*[to_vmem(a) for a in args])


def across(value, bits):
    return lax.ppermute(value, "x", [(i, i ^ bits) for i in range(lax.axis_size("x"))])


def swap(value, axes):
    return lax.all_to_all(value, axes, 0, 0)


def beside(value, axes, sends):
    if not sends:
        return swap(value, axes), []
    blocks, value = lax.optimization_barrier(([block for block, _ in sends], value))
    got = [across(block, bits) for block, (_, bits) in zip(blocks, sends)]
    return lax.optimization_barrier((swap(value, axes), got))


def sum_all(value, sends):
    value = swap(value, ("x", "core"))
    (value,) = call(fold_kernel, [in_vmem(lax.axis_size(("z", "y")), *value.shape[1:])], value)
    return beside(value, ("z", "y"), sends)


def other_core(value):
    return lax.ppermute(value, "core", [(0, 1), (1, 0)])


def sum_pairs(value, sends):
    row = in_vmem(1, value.shape[1])
    first, second = call(split_kernel, [row, row], value, other_core(value))
    pairs = (first, across(first, 3), second, across(second, 1))
    (value,) = call(join_kernel, [in_vmem(lax.axis_size(("z", "y")), *value.shape)], *pairs)
    return beside(value, ("z", "y"), sends)


def sum_rest(value, sends=()):
    if sends:
        blocks, value = lax.optimization_barrier(([block for block, _ in sends], value))
    got = [across(block, bits) for block, (_, bits) in zip(blocks, sends)] if sends else []
    (value,) = call(add_kernel, [in_vmem(lax.axis_size(("z", "y")), *value.shape)], value, other_core(value))
    value = swap(value, ("z", "y"))
    return lax.optimization_barrier((value, got)) if sends else (value, got)


def sum_along(part, axes):
    deep, wide, shape = lax.axis_size("z"), lax.axis_size(("x", "y")), part.shape[1:]
    (part,) = call(fold_kernel, [in_vmem(deep, *shape)], swap(part, axes))
    (part,) = call(fold_kernel, [in_vmem(wide, *shape)], swap(part, "z"))
    own = swap(part, ("x", "y")).reshape(wide * shape[0], shape[1])
    return own, other_core(own)


def sum_columns(keep, send):
    (part,) = call(add_kernel, [in_vmem(*keep.shape)], keep, other_core(send))
    count = lax.axis_size(("x", "y"))
    return sum_along(part.reshape(count, keep.shape[0] // count, keep.shape[1]), ("x", "y"))


def begin(points, rank, width, *args):
    tall, row = pltpu.VMEM((points, rank), F32), pltpu.VMEM((1, points), F32)
    packed = pltpu.VMEM((rank, 2 * width + LANES), F32)
    wide, block = in_vmem(points, width), in_vmem(rank + 8, points)
    half = in_vmem(rank // 2, 2 * width + LANES)
    return pl.pallas_call(
        begin_kernel,
        out_shape=[wide, wide, block, block, half, half],
        in_specs=[pl.BlockSpec(memory_space=pltpu.HBM)] * 6,
        scratch_shapes=[packed, tall, tall, row, row, pltpu.SemaphoreType.DMA((6,))],
        compiler_params=pltpu.CompilerParams(vmem_limit_bytes=VMEM),
    )(*[pltpu.with_memory_space_constraint(a, pltpu.HBM) for a in args])


def gradients(first, n, sums, before, near, blocks, axes):
    own, other = sums
    half, points = own.shape[0], near[0].shape[0]
    some, line = in_vmem(n, half, points), in_vmem(8, half)
    g1, g2, peak, small = call(
        lambda *refs: gradients_kernel(first, n, 0, *refs),
        [some, some, in_vmem(1, LANES), line],
        own,
        *before,
        *near,
        *blocks,
    )
    h1, h2, peak, more = call(
        lambda *refs: gradients_kernel(first, n, 1, *refs),
        [some, some, in_vmem(lax.axis_size(axes), 1, LANES), line],
        other,
        *before,
        peak,
        *near,
        *blocks,
    )
    return swap(peak, axes), g1, g2, small, h1, h2, more


def local(embed_source, embed_target, mass_source, mass_target, start_source, start_target):
    points, rank = start_source.shape
    width = embed_source.shape[1]
    sums_of, mid_of = in_vmem(2, rank), in_vmem(1, rank)
    sums_in = in_vmem(lax.axis_size(("x", "core")), 2, rank)
    block = in_vmem(rank + 8, points)
    x, y, w1, w2, keep, send = begin(
        points,
        rank,
        width,
        embed_source,
        embed_target,
        start_source,
        start_target,
        mass_source[None],
        mass_target[None],
    )
    found = gradients(True, 1, sum_columns(keep, send), (), (x, y), (w1, w2), AXES)
    k1, k2, kmid, sums = call(
        lambda *refs: first_step_kernel(True, 1, *refs), [block, block, mid_of, sums_in], *found, w1, w2
    )
    margins, (k1_1, k2_3) = sum_all(sums, [(k1, 1), (k2, 3)])
    pairs = (k1, k1_1, k2, k2_3)
    sums, scale = call(lambda *refs: step_kernel(True, 2, *refs), [sums_of, sums_of], margins, kmid, *pairs)
    margins, (k1_2, k2_2) = sum_pairs(sums, [(k1_1, 3), (k2_3, 1)])
    sums, scale = call(lambda *refs: step_kernel(False, 2, *refs), [sums_of, sums_of], margins, kmid, scale, *pairs)
    margins, (k1_3, k2_1) = sum_pairs(sums, [(k1, 3), (k2, 1)])
    blocks = (k1, k1_1, k1_3, k1_2, k2, k2_1, k2_3, k2_2)
    step = lambda *refs: step_kernel(False, 4, *refs)
    for inner in range(3, INNER - 1):
        sums, scale = call(step, [sums_of, sums_of], margins, kmid, scale, *blocks)
        if inner == 3:
            margins, (x_1, y_3) = sum_rest(sums, [(x, 1), (y, 3)])
        elif inner == 4:
            margins, (x_2, y_2) = sum_rest(sums, [(x_1, 3), (y_3, 1)])
        elif inner == 5:
            margins, (x_3, y_1) = sum_rest(sums, [(x, 3), (y, 1)])
        else:
            margins, _ = sum_rest(sums)
    near = (x, x_1, x_3, x_2, y, y_1, y_3, y_2)
    rest = ("core", "z", "y")
    for outer in range(1, OUTER):
        quarter = in_vmem(rank // lax.axis_size("x"), 2 * width + LANES)
        factor, scale, packed = call(
            last_step_kernel, [in_vmem(8, points), sums_of, quarter], margins, kmid, scale, *near, *blocks
        )
        count = lax.axis_size(("core", "y"))
        packed = packed.reshape(count, packed.shape[0] // count, packed.shape[1])
        found = gradients(False, 4, sum_along(packed, ("core", "y")), (scale, kmid), near, blocks, rest)
        *blocks, kmid, sums = call(
            lambda *refs: first_step_kernel(False, 4, *refs), [block] * 8 + [mid_of, sums_of], *found, factor, *blocks
        )
        margins, _ = sum_rest(sums)
        for inner in range(1, INNER - 1):
            before = () if inner == 1 else (scale,)
            sums, scale = call(
                lambda *refs: step_kernel(not before, 4, *refs), [sums_of, sums_of], margins, kmid, *before, *blocks
            )
            margins, _ = sum_rest(sums)
    sums, scale, factor = call(step, [sums_of, sums_of, in_vmem(2, points)], margins, kmid, scale, *blocks)
    margins, _ = sum_rest(sums)
    total = float(points * lax.axis_size(AXES) * rank)
    result = jax.ShapeDtypeStruct((points, rank), F32)
    left, right, middle = call(
        lambda *refs: end_kernel(total, *refs),
        [result, result, jax.ShapeDtypeStruct((1, rank), F32)],
        margins,
        kmid,
        scale,
        blocks[0],
        blocks[4],
        factor,
    )
    return left, right, middle[0]


def solution(mesh):
    mesh = Mesh(mesh.devices.reshape(4, 2, 8, 4), AXES)
    return jax.shard_map(
        local,
        mesh=mesh,
        in_specs=(P(AXES, None), P(AXES, None), P(AXES), P(AXES), P(AXES, None), P(AXES, None)),
        out_specs=(P(AXES, None), P(AXES, None), P()),
        check_vma=False,
    )
```
